256 devices in a mesh: dp: 32 (over y_hi, z, core), fsdp: 8 (over y_lo, x).
Axes of the slice: x: 4, y: 4 (y_hi: 2, y_lo: 2; y = y_hi * 2 + y_lo), z: 8, core: 2. Of those that a mesh axis runs over, the one named last changes fastest.
Arguments:
- feats: bfloat16 [16384, 1792], P(('dp', 'fsdp')), may hold values from -18 to 18
- proj_weight: bfloat16 [1792, 1152], P('fsdp'), may hold values from -0.125 to 0.125
- text_emb: bfloat16 [16384, 1152], P(('dp', 'fsdp')), may hold values from -18 to 18
- partner: int32 [16384], P('dp'), may hold values from 0 to 16383, each once
- log_scale: float32 [1], replicated, may hold values from 0.7 to 1.6
- bias: float32 [1], replicated, may hold values from -3 to -1
Outputs:
- grad_text: float32 [16384, 1152], P(('dp', 'fsdp'))
- grad_feats: bfloat16 [16384, 1792], P(('dp', 'fsdp'))
- grad_weight: float32 [1792, 1152], P('fsdp')
The draws below stay inside these ranges and needn't reach their ends.
Inputs may be any that keep to these rules, and one draw needn't show every extreme that they name: `partner`: each text matches exactly one image.
All inputs are finite; a program needn't handle non-finite values.
Results may differ from the reference program's by a relative error of at most 0.0064.
Values may be sent and summed in bfloat16 or wider, within the bound.
A program may use at most 64 MiB of HBM per device.

```python
import math
import jax
import jax.numpy as jnp
from jax import lax

D = 1792
EMBED = 1152
BATCH = 16384


def scaled_rows(key, row_total, col_total):
    key_scale, key_base = jax.random.split(key, 2)
    row_scale = jnp.exp(jax.random.uniform(key_scale, (row_total, 1), jnp.float32, jnp.log(0.3), jnp.log(3.0)))
    values = jnp.clip(jax.random.normal(key_base, (row_total, col_total), jnp.float32), -6.0, 6.0) * row_scale
    return values.astype(jnp.bfloat16)


def draw_feats(key, part):
    key = jax.random.fold_in(key, 13)
    return scaled_rows(key, BATCH, D)


def draw_text_emb(key, part):
    key = jax.random.fold_in(key, 11)
    return scaled_rows(key, BATCH, EMBED)


def shard_levels(stream_key, dims, cuts, low, top_value):
    factor_of = 1.0
    for position, parts in cuts:
        draws = jax.random.uniform(jax.random.fold_in(jax.random.fold_in(stream_key, 6), position), (parts,), jnp.float32, low / len(cuts), top_value / len(cuts))
        factor_of = factor_of * jnp.repeat(jnp.exp(draws), dims[position] // parts).reshape((-1,) + (1,) * (len(dims) - 1 - position))
    return factor_of


def bell_draw(stream_key, dims, spread, bound, cuts=(), kind=jnp.bfloat16):
    entries = jax.random.normal(stream_key, dims, jnp.float32) * spread
    if len(cuts) > 0:
        entries = shard_levels(stream_key, dims, cuts, -0.22, 0.18) * entries
    return jnp.clip(entries, min=-bound, max=bound).astype(kind)


def setup_inputs(seed: int = 0) -> dict:
    splits = jax.random.split(jax.random.key(seed), 7)
    return {
        "feats": draw_feats(jax.random.fold_in(splits[6], 71), 0),
        "proj_weight": bell_draw(splits[1], (D, EMBED), D ** -0.5, 0.125, ((0, 8),)),
        "text_emb": draw_text_emb(jax.random.fold_in(splits[6], 71), 0),
        "partner": jax.random.permutation(splits[3], BATCH).astype(jnp.int32),
        "log_scale": jnp.clip(jax.random.uniform(splits[4], (1,), jnp.float32, 0.7, 1.6), 0.7, 1.6),
        "bias": jnp.clip(jax.random.uniform(splits[5], (1,), jnp.float32, -3.0, -1.0), -3.0, -1.0),
    }


NORM_EPS = 1e-06

def normalize(values):
    inverse = lax.rsqrt(lax.optimization_barrier(jnp.sum(values * values, axis=-1, keepdims=True)) + NORM_EPS)
    return (values * inverse, inverse)

def reference(feats, proj_weight, text_emb, partner, log_scale, bias):
    logit_scale = jnp.exp(log_scale[0])
    logit_bias = bias[0]
    projected = jnp.dot(feats, proj_weight, preferred_element_type=jnp.float32)
    image_unit, image_inv = normalize(projected)
    image_half = image_unit.astype(jnp.bfloat16)
    text_unit, text_inv = normalize(text_emb.astype(jnp.float32))
    text_half = text_unit.astype(jnp.bfloat16)
    text_wide = text_half.astype(jnp.float32)
    block_rows = math.gcd(BATCH, 512)
    block_count = BATCH // block_rows
    image_blocks = image_half.astype(jnp.float32).reshape(block_count, block_rows, EMBED)
    partner_blocks = partner.reshape(block_count, block_rows)
    columns = jnp.arange(BATCH, dtype=jnp.int32)

    def pair_block(text_total, item):
        image_block, partner_block = item
        logits = logit_scale * jnp.dot(image_block, text_wide.T) + logit_bias
        sign = jnp.where(partner_block[:, None] == columns[None, :], jnp.float32(1.0), jnp.float32(-1.0))
        weight_pair = (-sign * jax.nn.sigmoid(-sign * logits)).astype(jnp.bfloat16).astype(jnp.float32)
        image_dir = logit_scale * jnp.dot(weight_pair, text_wide)
        text_total = text_total + jnp.dot(weight_pair.T, image_block)
        return (text_total, image_dir)
    text_total, image_dir = lax.scan(pair_block, jnp.zeros((BATCH, EMBED), jnp.float32), (image_blocks, partner_blocks))
    image_dir = image_dir.reshape(BATCH, EMBED)
    text_dir = logit_scale * text_total
    grad_text = text_inv * (text_dir - text_unit * lax.optimization_barrier(jnp.sum(text_unit * text_dir, axis=-1, keepdims=True)))
    proj_grad = (image_inv * (image_dir - image_unit * lax.optimization_barrier(jnp.sum(image_unit * image_dir, axis=-1, keepdims=True)))).astype(jnp.bfloat16)
    grad_feats = jnp.dot(proj_grad, proj_weight.T, preferred_element_type=jnp.float32).astype(jnp.bfloat16)
    grad_weight = jnp.dot(feats.T, proj_grad, preferred_element_type=jnp.float32)
    return (grad_text, grad_feats, grad_weight)
```

```python
import jax
import jax.numpy as jnp
from jax import lax
from jax.sharding import PartitionSpec as P

NORM_EPS = 1e-06


def normalize(values):
    inverse = lax.rsqrt(jnp.sum(values * values, axis=-1, keepdims=True) + NORM_EPS)
    return (values * inverse, inverse)


def body(feats, proj_weight, text_emb, partner, log_scale, bias):
    row_count = feats.shape[0]
    group_size = lax.axis_size("fsdp")
    loop_size = lax.axis_size("dp")
    column = lax.axis_index("fsdp")
    logit_scale = jnp.exp(log_scale[0])
    logit_bias = bias[0]
    text_unit, text_inv = normalize(text_emb.astype(jnp.float32))
    text_half = text_unit.astype(jnp.bfloat16)
    texts = lax.all_gather(text_half, "dp", axis=0, tiled=True)
    weight = lax.all_gather(proj_weight, "fsdp", axis=0, tiled=True)
    feats_cols = lax.all_to_all(feats, "fsdp", split_axis=1, concat_axis=0, tiled=True)
    projected = jnp.dot(feats, weight, preferred_element_type=jnp.float32)
    image_unit, image_inv = normalize(projected)
    images = lax.all_gather(image_unit.astype(jnp.bfloat16), "fsdp", axis=0, tiled=True)
    blocks = jnp.arange(loop_size, dtype=jnp.int32)
    text_index = (
        (blocks * group_size + column)[:, None] * row_count
        + jnp.arange(row_count, dtype=jnp.int32)[None, :]
    ).reshape(-1)
    dots = lax.dot_general(
        texts, images, (((1,), (1,)), ((), ())), preferred_element_type=jnp.float32
    )
    logits = logit_scale * dots + logit_bias
    sign = jnp.where(partner[None, :] == text_index[:, None], jnp.float32(1.0), jnp.float32(-1.0))
    weight_pair = (-sign * jax.nn.sigmoid(-sign * logits)).astype(jnp.bfloat16)
    image_part = lax.dot_general(
        weight_pair, texts, (((0,), (0,)), ((), ())), preferred_element_type=jnp.float32
    )
    image_dir = logit_scale * lax.psum_scatter(image_part, "fsdp", scatter_dimension=0, tiled=True)
    text_part = jnp.dot(weight_pair, images, preferred_element_type=jnp.float32)
    text_total = lax.psum_scatter(text_part, "dp", scatter_dimension=0, tiled=True)
    proj_grad = (
        image_inv
        * (image_dir - image_unit * jnp.sum(image_unit * image_dir, axis=-1, keepdims=True))
    ).astype(jnp.bfloat16)
    grads = lax.all_gather(proj_grad, "fsdp", axis=0, tiled=True)
    weight_shard = lax.dot_general(
        feats_cols, grads, (((0,), (0,)), ((), ())), preferred_element_type=jnp.float32
    )
    grad_weight = lax.psum(weight_shard, "dp")
    grad_feats = lax.dot_general(
        proj_grad, weight, (((1,), (1,)), ((), ())), preferred_element_type=jnp.float32
    ).astype(jnp.bfloat16)
    text_dir = logit_scale * text_total
    grad_text = text_inv * (
        text_dir - text_unit * jnp.sum(text_unit * text_dir, axis=-1, keepdims=True)
    )
    return (grad_text, grad_feats, grad_weight)


def solution(mesh):
    return jax.shard_map(
        body,
        mesh=mesh,
        in_specs=(
            P(("dp", "fsdp"), None),
            P("fsdp", None),
            P(("dp", "fsdp"), None),
            P("dp"),
            P(),
            P(),
        ),
        out_specs=(P(("dp", "fsdp"), None), P(("dp", "fsdp"), None), P("fsdp", None)),
        check_vma=False,
    )
```

```python
import functools

import jax
import jax.numpy as jnp
from jax import lax
from jax.experimental import pallas as pl
from jax.experimental.pallas import tpu as pltpu
from jax.sharding import PartitionSpec as P

NORM_EPS = 1e-06
MESH = pl.DeviceIdType.MESH
F32 = jnp.float32
BF16 = jnp.bfloat16
NT = (((1,), (1,)), ((), ()))
STOP = 99


def normalize(values):
    inverse = lax.rsqrt(jnp.sum(values * values, axis=-1, keepdims=True) + NORM_EPS)
    return (values * inverse, inverse)


def kernel(
    zs,
    xs,
    feats,
    wshard,
    text_emb,
    partner,
    log_scale,
    bias,
    grad_text,
    grad_feats,
    grad_weight,
    texts,
    wfull,
    images,
    fsplit,
    fgroup,
    fturned,
    proj,
    tpart,
    tsib,
    image_acc,
    ring_in,
    ring_out,
    yout,
    yin,
    iout,
    iin,
    grads,
    gw,
    gout,
    gsib,
    zout,
    zin,
    gyout,
    gyin,
    fin,
    send,
    recv,
):
    rows, embed = text_emb.shape
    wrows = wshard.shape[0]
    whalf = wrows // 2
    group = 2 * xs
    pair = 2 * rows
    unit = 4 * rows
    p = lax.axis_index("dp")
    f = lax.axis_index("fsdp")
    core = lax.rem(p, 2)
    z = lax.rem(p // 2, zs)
    yh = p // (2 * zs)
    x = lax.rem(f, xs)
    yl = f // xs

    def at_z(zz):
        return (yh * (2 * zs) + zz * 2 + core, f)

    def zplus(by):
        return lax.rem(z + by + zs, zs)

    sib = (p + 1 - 2 * core, f)
    across = (p + 2 * zs * (1 - 2 * yh), f)

    def peer(k):
        dy, dx = k // xs, k % xs
        to_y = 1 - yl if dy else yl
        return to_y * xs + lax.rem(x + dx, xs)

    def source(k):
        dy, dx = k // xs, k % xs
        to_y = 1 - yl if dy else yl
        return to_y * xs + lax.rem(x + xs - dx, xs)

    used = [0]
    pending = []

    def ids(count):
        first = used[0]
        used[0] += count
        return first

    def copy(src, dst, i, device):
        return pltpu.make_async_remote_copy(
            src_ref=src,
            dst_ref=dst,
            send_sem=send.at[i],
            recv_sem=recv.at[i],
            device_id=device,
            device_id_type=MESH,
        )

    def start(src, dst, i, device):
        c = copy(src, dst, i, device)
        c.start()
        pending.append(c)
        return c

    group_ks = [k for k in (1, xs - 1, 2, xs, xs + 1, 2 * xs - 1, xs + 2) if k < group]
    group_ks = list(dict.fromkeys(group_ks))
    assert len(group_ks) == group - 1

    barrier = pltpu.get_barrier_semaphore()
    others = [sib, across]
    others += [at_z(zplus(k)) for k in range(1, zs)]
    others += [(p, peer(k)) for k in range(1, group)]
    for device in others:
        pl.semaphore_signal(barrier, inc=1, device_id=device, device_id_type=MESH)
    pl.semaphore_wait(barrier, len(others))

    own_half = pl.ds(pl.multiple_of(core * whalf, 16), whalf)
    wid = ids(group)
    wcopies = {}
    for k in group_ks:
        wcopies[k] = start(wshard.at[own_half], wfull.at[f, own_half], wid + k, (p, peer(k)))

    text_unit, text_inv = normalize(text_emb[...].astype(F32))
    mine = pl.ds(pl.multiple_of(core * pair + yh * rows, 16), rows)
    own_pair = pl.ds(pl.multiple_of(core * pair, 16), pair)
    sib_pair = pl.ds(pl.multiple_of((1 - core) * pair, 16), pair)
    texts[z, mine] = text_unit.astype(BF16)
    ty = start(texts.at[z, mine], texts.at[z, mine], ids(1), across)

    for j in range(group):
        fsplit[j] = feats[:, j * wrows : (j + 1) * wrows]
    wfull[f] = wshard[...]
    proj[...] = jnp.dot(fsplit[f], wshard[...], preferred_element_type=F32)

    half = zs // 2
    rid, lid, tsid = ids(half), ids(half), ids(2 * half)
    ring_r, ring_l, text_sib = [], [], []
    low = pl.ds(pl.multiple_of(core * pair, 16), rows)
    high = pl.ds(pl.multiple_of(core * pair + rows, 16), rows)

    def text_step(s):
        a = low if s == half - 1 else own_pair
        b = high if s == half - 1 else own_pair
        ur, ul = zplus(-s), zplus(s)
        ring_r.append(start(texts.at[ur, a], texts.at[ur, a], rid + s, at_z(zplus(1))))
        ring_l.append(start(texts.at[ul, b], texts.at[ul, b], lid + s, at_z(zplus(-1))))

    def to_sib(u, i):
        text_sib.append(start(texts.at[u, own_pair], texts.at[u, own_pair], tsid + i, sib))

    def text_arrive(s):
        ring_r[s].wait_recv()
        ring_l[s].wait_recv()
        if s < half - 1:
            text_step(s + 1)
            to_sib(zplus(-1 - s), 2 * s + 1)
            to_sib(zplus(1 + s), 2 * s + 2)
        else:
            to_sib(zplus(half), 2 * s + 1)

    ty.wait_recv()
    text_step(0)
    to_sib(z, 0)

    wsid = ids(group)
    wsib = []

    def weight_arrive(k):
        wcopies[k].wait_recv()
        a = wfull.at[source(k), own_half]
        wsib.append((k, start(a, a, wsid + k, sib)))

    def weight_use(i):
        k, c = wsib[i]
        c.wait_recv()
        j = source(k)
        proj[...] += jnp.dot(fsplit[j], wfull[j], preferred_element_type=F32)

    plan = {min(2 * s + 1, group - 2): s for s in range(half - 1)}
    for i, k in enumerate(group_ks):
        weight_arrive(k)
        if i:
            weight_use(i - 1)
        if i in plan:
            text_arrive(plan[i])
    weight_use(len(group_ks) - 1)

    image_unit, image_inv = normalize(proj[...])
    images[f] = image_unit.astype(BF16)
    iid = ids(group)
    icopies = [start(images.at[f], images.at[f], iid + k, (p, peer(k))) for k in group_ks]
    text_arrive(half - 1)
    image_acc[...] = jnp.zeros_like(image_acc)
    for c in text_sib:
        c.wait_recv()
    for c in icopies:
        c.wait_recv()

    fid = ids(group)
    fcopies = [start(fsplit.at[peer(k)], fgroup.at[f], fid + k, (p, peer(k))) for k in group_ks]
    fgroup[f] = fsplit[f]

    image_rows = images[...].reshape(group * rows, embed)
    scale = jnp.exp(log_scale[...])
    shift = bias[...]
    tpid = ids(zs)

    def part_copy(k):
        return copy(tpart.at[k, sib_pair], tsib.at[k], tpid + k, sib)

    def pairs(k, carry):
        d = half - (k + 1) // 2
        u = lax.rem(z + jnp.where(lax.rem(k, 2) == 1, d, zs - d), zs)
        block = texts[u]
        dots = lax.dot_general(block, image_rows, NT, preferred_element_type=F32)
        logits = scale * dots + shift
        r = lax.broadcasted_iota(jnp.int32, (unit, 1), 0)
        c_of = r // pair
        y_of = lax.rem(r // rows, 2)
        index = ((y_of * (2 * zs) + u * 2 + c_of) * group + f) * rows + lax.rem(r, rows)
        chance = 1.0 / (1.0 + jnp.exp(-logits))
        weight = jnp.where(partner[...] == index, chance - 1.0, chance).astype(BF16)
        tpart[k] = jnp.dot(weight, image_rows, preferred_element_type=F32).astype(BF16)
        part_copy(k).start()
        image_acc[...] += jnp.dot(weight.T, block, preferred_element_type=F32)
        return carry

    rsid, lsid = ids(half), ids(half)
    sum_r, sum_l = [], []

    def own_sum(k, lo, count):
        at = pl.ds(pl.multiple_of(core * pair + lo, 16), count)
        return tpart[k, at].astype(F32) + tsib[k, lo : lo + count].astype(F32)

    def sum_step(s):
        kr, kl = (0, 0) if s == 0 else (2 * s - 1, 2 * s)
        for k in range(0 if s == 0 else kr, kl + 1):
            part_copy(k).wait_recv()
        if s:
            sum_r[s - 1].wait_recv()
            sum_l[s - 1].wait_recv()
        if s == 0:
            ring_out[0, 0, :rows] = own_sum(0, 0, rows).astype(BF16)
            ring_out[1, 0, rows:] = own_sum(0, rows, rows).astype(BF16)
            a, b = pl.ds(0, rows), pl.ds(rows, rows)
        elif s == 1:
            ring_out[0, 1, :rows] = (own_sum(kr, 0, rows) + ring_in[0, 0, :rows].astype(F32)).astype(BF16)
            ring_out[0, 1, rows:] = own_sum(kr, rows, rows).astype(BF16)
            ring_out[1, 1, :rows] = own_sum(kl, 0, rows).astype(BF16)
            ring_out[1, 1, rows:] = (own_sum(kl, rows, rows) + ring_in[1, 0, rows:].astype(F32)).astype(BF16)
            a = b = pl.ds(0, pair)
        else:
            ring_out[0, s] = (own_sum(kr, 0, pair) + ring_in[0, s - 1].astype(F32)).astype(BF16)
            ring_out[1, s] = (own_sum(kl, 0, pair) + ring_in[1, s - 1].astype(F32)).astype(BF16)
            a = b = pl.ds(0, pair)
        sum_r.append(start(ring_out.at[0, s, a], ring_in.at[0, s, a], rsid + s, at_z(zplus(1))))
        sum_l.append(start(ring_out.at[1, s, b], ring_in.at[1, s, b], lsid + s, at_z(zplus(-1))))

    pairs(0, 0)
    lax.fori_loop(1, 3, pairs, 0)
    sum_step(0)
    lax.fori_loop(3, zs, pairs, 0)

    iout[...] = image_acc[...].reshape(group, rows, embed).astype(BF16)
    isid = ids(group)
    iscopies = [start(iout.at[peer(k)], iin.at[k], isid + k, (p, peer(k))) for k in group_ks]
    sum_step(1)
    for c in fcopies:
        c.wait_recv()
    fturned[...] = fgroup[...].reshape(group * rows, wrows).T
    total = image_acc[pl.ds(pl.multiple_of(f * rows, 8), rows)]
    for k, c in zip(group_ks, iscopies):
        c.wait_recv()
        total += iin[k].astype(F32)
    image_dir = scale * total
    image_unit, image_inv = normalize(proj[...])
    along = jnp.sum(image_unit * image_dir, axis=-1, keepdims=True)
    grads[f] = (image_inv * (image_dir - image_unit * along)).astype(BF16)
    gid = ids(group)
    gcopies = [start(grads.at[f], grads.at[f], gid + k, (p, peer(k))) for k in group_ks]

    sum_step(2)
    own_grads = grads[f]
    for j in range(group):
        grad_feats[:, j * wrows : (j + 1) * wrows] = lax.dot_general(
            own_grads, wfull[j], NT, preferred_element_type=F32
        ).astype(BF16)
    for s in range(3, half):
        sum_step(s)

    for c in gcopies:
        c.wait_recv()
    gw[...] = jnp.dot(
        fturned[...], grads[...].reshape(group * rows, embed), preferred_element_type=F32
    )
    gout[...] = gw[...].astype(BF16)
    other_half = pl.ds(pl.multiple_of((1 - core) * whalf, 16), whalf)
    gs = start(gout.at[other_half], gsib, ids(1), sib)
    part = zout.shape[1]
    used_parts = whalf // part
    gs.wait_recv()
    zout[:used_parts] = (gw[own_half] + gsib[...].astype(F32)).astype(BF16).reshape(
        used_parts, part, embed
    )
    for j in range(used_parts, zs):
        zout[j] = jnp.zeros_like(zout[j])
    zid = ids(zs)
    zcopies = [
        start(zout.at[zplus(k)], zin.at[k], zid + k, at_z(zplus(k))) for k in range(1, zs)
    ]

    part_copy(zs - 1).wait_recv()
    sum_r[half - 1].wait_recv()
    sum_l[half - 1].wait_recv()
    theirs = pl.ds(pl.multiple_of((1 - yh) * rows, 16), rows)
    ours = pl.ds(pl.multiple_of(yh * rows, 16), rows)

    def gathered(at, lo):
        here = pl.ds(pl.multiple_of(core * pair + lo, 16), rows)
        return (
            (tpart[zs - 1, here].astype(F32) + tsib[zs - 1, at].astype(F32))
            + (ring_in[0, half - 1, at].astype(F32) + ring_in[1, half - 1, at].astype(F32))
        )

    yout[...] = gathered(theirs, (1 - yh) * rows).astype(BF16)
    yc = start(yout, yin, ids(1), across)

    weight_sum = zout[z].astype(F32)
    for k, c in zip(range(1, zs), zcopies):
        c.wait_recv()
        weight_sum += zin[k].astype(F32)
    gyout[...] = weight_sum.astype(BF16)
    gy = start(gyout, gyin, ids(1), across)

    yc.wait_recv()
    text_dir = scale * (gathered(ours, yh * rows) + yin[...].astype(F32))
    text_unit, text_inv = normalize(text_emb[...].astype(F32))
    along = jnp.sum(text_unit * text_dir, axis=-1, keepdims=True)
    grad_text[...] = text_inv * (text_dir - text_unit * along)

    gy.wait_recv()
    fin[core, z] = (gyout[...].astype(F32) + gyin[...].astype(F32)).astype(BF16)
    finid = ids(zs)
    fincopies = [
        start(fin.at[core, z], fin.at[core, z], finid + k, at_z(zplus(k))) for k in range(1, zs)
    ]
    for c in fincopies:
        c.wait_recv()
    fs = start(fin.at[core], fin.at[core], ids(1), sib)
    fs.wait_recv()
    for c in range(2):
        grad_weight[c * whalf : (c + 1) * whalf] = (
            fin[c, :used_parts].reshape(whalf, embed).astype(F32)
        )

    for c in pending:
        c.wait_send()

    def part_done(k, carry):
        part_copy(k).wait_send()
        return carry

    lax.fori_loop(0, zs, part_done, 0)


SEMS = 128


def body(zs, xs, feats, proj_weight, text_emb, partner, log_scale, bias):
    rows, width = feats.shape
    wrows, embed = proj_weight.shape
    group = 2 * xs
    pair, unit = 2 * rows, 4 * rows
    half = zs // 2
    whalf = wrows // 2
    part = -(-whalf // zs // 16) * 16
    vmem = pl.BlockSpec(memory_space=pltpu.VMEM)
    scratch = [
        ((zs, unit, embed), BF16),
        ((group, wrows, embed), BF16),
        ((group, rows, embed), BF16),
        ((group, rows, wrows), BF16),
        ((group, rows, wrows), BF16),
        ((wrows, group * rows), BF16),
        ((rows, embed), F32),
        ((zs, unit, embed), BF16),
        ((zs, pair, embed), BF16),
        ((group * rows, embed), F32),
        ((2, half, pair, embed), BF16),
        ((2, half, pair, embed), BF16),
        ((rows, embed), BF16),
        ((rows, embed), BF16),
        ((group, rows, embed), BF16),
        ((group, rows, embed), BF16),
        ((group, rows, embed), BF16),
        ((wrows, embed), F32),
        ((wrows, embed), BF16),
        ((whalf, embed), BF16),
        ((zs, part, embed), BF16),
        ((zs, part, embed), BF16),
        ((part, embed), BF16),
        ((part, embed), BF16),
        ((2, zs, part, embed), BF16),
    ]
    return pl.pallas_call(
        functools.partial(kernel, zs, xs),
        out_shape=(
            jax.ShapeDtypeStruct((rows, embed), F32),
            jax.ShapeDtypeStruct((rows, width), BF16),
            jax.ShapeDtypeStruct((wrows, embed), F32),
        ),
        in_specs=[vmem] * 6,
        out_specs=(vmem,) * 3,
        scratch_shapes=[pltpu.VMEM(shape, kind) for shape, kind in scratch]
        + [pltpu.SemaphoreType.DMA((SEMS,)), pltpu.SemaphoreType.DMA((SEMS,))],
        compiler_params=pltpu.CompilerParams(
            collective_id=0, has_side_effects=True, vmem_limit_bytes=56 * 2**20
        ),
    )(
        feats,
        proj_weight,
        text_emb,
        partner.reshape(1, group * rows),
        log_scale.reshape(1, 1),
        bias.reshape(1, 1),
    )


def solution(mesh):
    zs = mesh.shape["dp"] // 4
    xs = mesh.shape["fsdp"] // 2
    return jax.shard_map(
        functools.partial(body, zs, xs),
        mesh=mesh,
        in_specs=(
            P(("dp", "fsdp"), None),
            P("fsdp", None),
            P(("dp", "fsdp"), None),
            P("dp"),
            P(),
            P(),
        ),
        out_specs=(P(("dp", "fsdp"), None), P(("dp", "fsdp"), None), P("fsdp", None)),
        check_vma=False,
    )
```

```python
import functools

import jax
import jax.numpy as jnp
from jax import lax
from jax.experimental import pallas as pl
from jax.experimental.pallas import tpu as pltpu
from jax.sharding import PartitionSpec as P

NORM_EPS = 1e-06
MESH = pl.DeviceIdType.MESH
F32 = jnp.float32
BF16 = jnp.bfloat16
NT = (((1,), (1,)), ((), ()))
STOP = 99


def normalize(values):
    inverse = lax.rsqrt(jnp.sum(values * values, axis=-1, keepdims=True) + NORM_EPS)
    return (values * inverse, inverse)


def kernel(
    zs,
    xs,
    feats,
    wshard,
    text_emb,
    partner,
    log_scale,
    bias,
    grad_text,
    grad_feats,
    grad_weight,
    texts,
    images,
    fsplit,
    fgroup,
    fturned,
    pacc,
    pout,
    pin,
    proj,
    pbuf,
    wbuf,
    tpart,
    tsib,
    image_acc,
    ring_in,
    ring_out,
    yout,
    yin,
    iout,
    iin,
    grads,
    gfout,
    gfin,
    gw,
    gout,
    gsib,
    zout,
    zin,
    gyout,
    gyin,
    fin,
    send,
    recv,
):
    rows, embed = text_emb.shape
    wrows = wshard.shape[0]
    whalf = wrows // 2
    group = 2 * xs
    part_rows = rows // 2
    image_half = group * part_rows
    pair = 2 * rows
    unit = 4 * rows
    half = zs // 2
    p = lax.axis_index("dp")
    f = lax.axis_index("fsdp")
    core = lax.rem(p, 2)
    z = lax.rem(p // 2, zs)
    yh = p // (2 * zs)
    x = lax.rem(f, xs)
    yl = f // xs

    def at_z(zz):
        return (yh * (2 * zs) + zz * 2 + core, f)

    def zplus(by):
        return lax.rem(z + by + zs, zs)

    sib = (p + 1 - 2 * core, f)
    across = (p + 2 * zs * (1 - 2 * yh), f)

    def peer(k):
        dy, dx = k // xs, k % xs
        to_y = 1 - yl if dy else yl
        return to_y * xs + lax.rem(x + dx, xs)

    used = [0]
    pending = []

    def ids(count):
        first = used[0]
        used[0] += count
        return first

    def copy(src, dst, i, device):
        return pltpu.make_async_remote_copy(
            src_ref=src,
            dst_ref=dst,
            send_sem=send.at[i],
            recv_sem=recv.at[i],
            device_id=device,
            device_id_type=MESH,
        )

    def start(src, dst, i, device):
        c = copy(src, dst, i, device)
        c.start()
        pending.append(c)
        return c

    group_ks = [k for k in (1, xs - 1, xs, 2, xs + 1, 2 * xs - 1, xs + 2) if k < group]
    group_ks = list(dict.fromkeys(group_ks))
    assert len(group_ks) == group - 1

    def to_group(src, dst):
        first = ids(group)
        return [start(src(k), dst(k), first + k, (p, peer(k))) for k in group_ks]

    def wait_all(copies):
        for c in copies:
            c.wait_recv()

    barrier = pltpu.get_barrier_semaphore()
    others = [sib, across]
    others += [at_z(zplus(k)) for k in range(1, zs)]
    others += [(p, peer(k)) for k in range(1, group)]
    for device in others:
        pl.semaphore_signal(barrier, inc=1, device_id=device, device_id_type=MESH)
    pl.semaphore_wait(barrier, len(others))

    for j in range(group):
        fsplit[j] = feats[:, j * wrows : (j + 1) * wrows]
    fcopies = to_group(lambda k: fsplit.at[peer(k)], lambda k: fgroup.at[f])

    text_unit, text_inv = normalize(text_emb[...].astype(F32))

    def chunk(q):
        y = yh if q == 0 else 1 - yh
        return pl.ds(pl.multiple_of(core * pair + y * rows, 16), rows)

    texts[z, chunk(0)] = text_unit.astype(BF16)
    own_text = texts.at[z, chunk(0)]
    ty = start(own_text, own_text, ids(1), across)
    ring = {}
    text_sib = {}

    def ring_send(way, s, q):
        u = zplus(-way * s)
        a = texts.at[u, chunk(q)]
        ring[way, s, q] = start(a, a, ids(1), at_z(zplus(way)))

    def to_sib(by, q):
        a = texts.at[zplus(by), chunk(q)]
        text_sib.setdefault(by, []).append(start(a, a, ids(1), sib))

    def arrive(s, q):
        for way in (1, -1):
            if (way, s, q) not in ring:
                continue
            ring[way, s, q].wait_recv()
            if s < half - 2 or (s == half - 2 and q == (0 if way == 1 else 1)):
                ring_send(way, s + 1, q)
            by = -way * (s + 1)
            to_sib(half if by == -half else by, q)

    def text_ready(by):
        wait_all(text_sib[by])

    ring_send(1, 0, 0)
    ring_send(-1, 0, 0)
    to_sib(0, 0)
    fgroup[f] = fsplit[f]
    for h in range(2):
        for j in range(group):
            lane = j * rows + h * part_rows
            pbuf[h, :, j * part_rows : (j + 1) * part_rows] = partner[:, lane : lane + part_rows]
    ty.wait_recv()
    ring_send(1, 0, 1)
    ring_send(-1, 0, 1)
    to_sib(0, 1)

    wait_all(fcopies)
    pcopies = []
    for h in range(2):
        cols = fgroup[:, h * part_rows : (h + 1) * part_rows].reshape(image_half, wrows)
        pacc[h] = jnp.dot(cols, wshard[...], preferred_element_type=F32)
        pout[h] = pacc[h].reshape(group, part_rows, embed).astype(BF16)
        pcopies.append(to_group(lambda k: pout.at[h, peer(k)], lambda k: pin.at[h, k]))
    for h in range(2):
        cols = fgroup[:, h * part_rows : (h + 1) * part_rows].reshape(image_half, wrows)
        fturned[h] = cols.T
    image_acc[...] = jnp.zeros_like(image_acc)
    arrive(0, 0)
    arrive(0, 1)

    def own_rows(ref, h):
        return ref[h, pl.ds(pl.multiple_of(f * part_rows, 16), part_rows)]

    icopies = []

    def project(h):
        total = own_rows(pacc, h)
        wait_all(pcopies[h])
        for k in group_ks:
            total += pin[h, k].astype(F32)
        proj[h] = total
        images[h, f] = normalize(total)[0].astype(BF16)
        icopies.append(to_group(lambda k: images.at[h, f], lambda k: images.at[h, f]))

    project(0)
    arrive(1, 0)
    project(1)
    arrive(1, 1)

    scale = jnp.exp(log_scale[...])
    shift = bias[...]

    def front(u, h):
        block = texts[u]
        image_rows = images[h].reshape(image_half, embed)
        dots = lax.dot_general(block, image_rows, NT, preferred_element_type=F32)
        logits = scale * dots + shift
        r = lax.broadcasted_iota(jnp.int32, (unit, 1), 0)
        c_of = r // pair
        y_of = lax.rem(r // rows, 2)
        index = ((y_of * (2 * zs) + u * 2 + c_of) * group + f) * rows + lax.rem(r, rows)
        chance = 1.0 / (1.0 + jnp.exp(-logits))
        weight = jnp.where(pbuf[h] == index, chance - 1.0, chance).astype(BF16)
        wbuf[u, :, h * image_half : (h + 1) * image_half] = weight
        image_acc[h] += jnp.dot(weight.T, block, preferred_element_type=F32)

    def two_sides(by):
        def one(i, carry):
            front(lax.rem(z + zs + by * (2 * i - 1), zs), 0)
            return carry

        lax.fori_loop(0, 2, one, 0)

    iscopies = []

    def image_sums(h):
        iout[h] = image_acc[h].reshape(group, part_rows, embed).astype(BF16)
        iscopies.append(to_group(lambda k: iout.at[h, peer(k)], lambda k: iin.at[h, k]))

    text_ready(0)
    wait_all(icopies[0])
    front(z, 0)
    for s in range(1, half):
        if s + 1 < half:
            arrive(s + 1, 0)
            arrive(s + 1, 1)
        text_ready(-s)
        text_ready(s)
        two_sides(s)
    text_ready(half)
    front(zplus(half), 0)
    image_sums(0)
    wait_all(icopies[1])

    def second(u, carry):
        front(u, 1)
        return carry

    lax.fori_loop(0, zs, second, 0)
    image_sums(1)

    tpid = ids(zs)
    sib_pair = pl.ds(pl.multiple_of((1 - core) * pair, 16), pair)

    def part_copy(k):
        return copy(tpart.at[k, sib_pair], tsib.at[k], tpid + k, sib)

    def back(k, carry):
        d = half - (k + 1) // 2
        u = lax.rem(z + jnp.where(lax.rem(k, 2) == 1, d, zs - d), zs)
        image_rows = images[...].reshape(2 * image_half, embed)
        tpart[k] = jnp.dot(wbuf[u], image_rows, preferred_element_type=F32).astype(BF16)
        part_copy(k).start()
        return carry

    rsid, lsid = ids(half), ids(half)
    sum_r, sum_l = [], []

    def own_sum(k, lo, count):
        at = pl.ds(pl.multiple_of(core * pair + lo, 16), count)
        return tpart[k, at].astype(F32) + tsib[k, lo : lo + count].astype(F32)

    def sum_step(s):
        kr, kl = (0, 0) if s == 0 else (2 * s - 1, 2 * s)
        for k in range(0 if s == 0 else kr, kl + 1):
            part_copy(k).wait_recv()
        if s:
            sum_r[s - 1].wait_recv()
            sum_l[s - 1].wait_recv()
        if s == 0:
            ring_out[0, 0, :rows] = own_sum(0, 0, rows).astype(BF16)
            ring_out[1, 0, rows:] = own_sum(0, rows, rows).astype(BF16)
            a, b = pl.ds(0, rows), pl.ds(rows, rows)
        elif s == 1:
            ring_out[0, 1, :rows] = (own_sum(kr, 0, rows) + ring_in[0, 0, :rows].astype(F32)).astype(BF16)
            ring_out[0, 1, rows:] = own_sum(kr, rows, rows).astype(BF16)
            ring_out[1, 1, :rows] = own_sum(kl, 0, rows).astype(BF16)
            ring_out[1, 1, rows:] = (own_sum(kl, rows, rows) + ring_in[1, 0, rows:].astype(F32)).astype(BF16)
            a = b = pl.ds(0, pair)
        else:
            ring_out[0, s] = (own_sum(kr, 0, pair) + ring_in[0, s - 1].astype(F32)).astype(BF16)
            ring_out[1, s] = (own_sum(kl, 0, pair) + ring_in[1, s - 1].astype(F32)).astype(BF16)
            a = b = pl.ds(0, pair)
        sum_r.append(start(ring_out.at[0, s, a], ring_in.at[0, s, a], rsid + s, at_z(zplus(1))))
        sum_l.append(start(ring_out.at[1, s, b], ring_in.at[1, s, b], lsid + s, at_z(zplus(-1))))

    lax.fori_loop(0, 2, back, 0)
    sum_step(0)
    lax.fori_loop(2, zs, back, 0)

    gcopies = []

    def project_back(h):
        total = own_rows(image_acc, h)
        wait_all(iscopies[h])
        for k in group_ks:
            total += iin[h, k].astype(F32)
        image_dir = scale * total
        image_unit, image_inv = normalize(proj[h])
        along = jnp.sum(image_unit * image_dir, axis=-1, keepdims=True)
        grads[h, f] = (image_inv * (image_dir - image_unit * along)).astype(BF16)
        gcopies.append(to_group(lambda k: grads.at[h, f], lambda k: grads.at[h, f]))

    project_back(0)
    sum_step(1)
    project_back(1)
    sum_step(2)

    wait_all(gcopies[0])
    gw[...] = jnp.dot(
        fturned[0], grads[0].reshape(image_half, embed), preferred_element_type=F32
    )
    wait_all(gcopies[1])
    gw[...] += jnp.dot(
        fturned[1], grads[1].reshape(image_half, embed), preferred_element_type=F32
    )
    gout[...] = gw[...].astype(BF16)
    own_half = pl.ds(pl.multiple_of(core * whalf, 16), whalf)
    other_half = pl.ds(pl.multiple_of((1 - core) * whalf, 16), whalf)
    gs = start(gout.at[other_half], gsib, ids(1), sib)
    part = zout.shape[1]
    used_parts = whalf // part
    for j in range(used_parts, zs):
        zout[j] = jnp.zeros_like(zout[j])
    gs.wait_recv()
    zout[:used_parts] = (gw[own_half] + gsib[...].astype(F32)).astype(BF16).reshape(
        used_parts, part, embed
    )
    zid = ids(zs)
    zcopies = [
        start(zout.at[zplus(k)], zin.at[k], zid + k, at_z(zplus(k))) for k in range(1, zs)
    ]

    gfcopies = []
    for h in range(2):
        cols = lax.dot_general(
            grads[h].reshape(image_half, embed), wshard[...], NT, preferred_element_type=F32
        )
        gfout[h] = cols.astype(BF16).reshape(group, part_rows, wrows)
        gfcopies += to_group(lambda k: gfout.at[h, peer(k)], lambda k: gfin.at[h, f])
        gfin[h, f] = gfout[h, f]
    for s in range(3, half):
        sum_step(s)

    weight_sum = zout[z].astype(F32)
    for k, c in zip(range(1, zs), zcopies):
        c.wait_recv()
        weight_sum += zin[k].astype(F32)
    gyout[...] = weight_sum.astype(BF16)
    gy = start(gyout, gyin, ids(1), across)
    wait_all(gfcopies)
    for h in range(2):
        for j in range(group):
            at = (slice(h * part_rows, (h + 1) * part_rows), slice(j * wrows, (j + 1) * wrows))
            grad_feats[at] = gfin[h, j]
    gy.wait_recv()
    fin[core, z] = (gyout[...].astype(F32) + gyin[...].astype(F32)).astype(BF16)
    finid = ids(zs)
    fincopies = [
        start(fin.at[core, z], fin.at[core, z], finid + k, at_z(zplus(k))) for k in range(1, zs)
    ]

    part_copy(zs - 1).wait_recv()
    sum_r[half - 1].wait_recv()
    sum_l[half - 1].wait_recv()
    theirs = pl.ds(pl.multiple_of((1 - yh) * rows, 16), rows)
    ours = pl.ds(pl.multiple_of(yh * rows, 16), rows)

    def gathered(at, lo):
        here = pl.ds(pl.multiple_of(core * pair + lo, 16), rows)
        return (
            (tpart[zs - 1, here].astype(F32) + tsib[zs - 1, at].astype(F32))
            + (ring_in[0, half - 1, at].astype(F32) + ring_in[1, half - 1, at].astype(F32))
        )

    yout[...] = gathered(theirs, (1 - yh) * rows).astype(BF16)
    yc = start(yout, yin, ids(1), across)
    wait_all(fincopies)
    fs = start(fin.at[core], fin.at[core], ids(1), sib)
    yc.wait_recv()
    text_dir = scale * (gathered(ours, yh * rows) + yin[...].astype(F32))
    text_unit, text_inv = normalize(text_emb[...].astype(F32))
    along = jnp.sum(text_unit * text_dir, axis=-1, keepdims=True)
    grad_text[...] = text_inv * (text_dir - text_unit * along)
    fs.wait_recv()
    for c in range(2):
        grad_weight[c * whalf : (c + 1) * whalf] = (
            fin[c, :used_parts].reshape(whalf, embed).astype(F32)
        )

    for c in pending:
        c.wait_send()

    def part_done(k, carry):
        part_copy(k).wait_send()
        return carry

    lax.fori_loop(0, zs, part_done, 0)


SEMS = 192


def body(zs, xs, feats, proj_weight, text_emb, partner, log_scale, bias):
    rows, width = feats.shape
    wrows, embed = proj_weight.shape
    group = 2 * xs
    pair, unit = 2 * rows, 4 * rows
    half = zs // 2
    whalf = wrows // 2
    part_rows = rows // 2
    image_half = group * part_rows
    part = -(-whalf // zs // 16) * 16
    vmem = pl.BlockSpec(memory_space=pltpu.VMEM)
    halves = ((2, group, part_rows, embed), BF16)
    scratch = [
        ((zs, unit, embed), BF16),
        halves,
        ((group, rows, wrows), BF16),
        ((group, rows, wrows), BF16),
        ((2, wrows, image_half), BF16),
        ((2, image_half, embed), F32),
        halves,
        halves,
        ((2, part_rows, embed), F32),
        ((2, 1, image_half), jnp.int32),
        ((zs, unit, 2 * image_half), BF16),
        ((zs, unit, embed), BF16),
        ((zs, pair, embed), BF16),
        ((2, image_half, embed), F32),
        ((2, half, pair, embed), BF16),
        ((2, half, pair, embed), BF16),
        ((rows, embed), BF16),
        ((rows, embed), BF16),
        halves,
        halves,
        halves,
        ((2, group, part_rows, wrows), BF16),
        ((2, group, part_rows, wrows), BF16),
        ((wrows, embed), F32),
        ((wrows, embed), BF16),
        ((whalf, embed), BF16),
        ((zs, part, embed), BF16),
        ((zs, part, embed), BF16),
        ((part, embed), BF16),
        ((part, embed), BF16),
        ((2, zs, part, embed), BF16),
    ]
    return pl.pallas_call(
        functools.partial(kernel, zs, xs),
        out_shape=(
            jax.ShapeDtypeStruct((rows, embed), F32),
            jax.ShapeDtypeStruct((rows, width), BF16),
            jax.ShapeDtypeStruct((wrows, embed), F32),
        ),
        in_specs=[vmem] * 6,
        out_specs=(vmem,) * 3,
        scratch_shapes=[pltpu.VMEM(shape, kind) for shape, kind in scratch]
        + [pltpu.SemaphoreType.DMA((SEMS,)), pltpu.SemaphoreType.DMA((SEMS,))],
        compiler_params=pltpu.CompilerParams(
            collective_id=0, has_side_effects=True, vmem_limit_bytes=56 * 2**20
        ),
    )(
        feats,
        proj_weight,
        text_emb,
        partner.reshape(1, group * rows),
        log_scale.reshape(1, 1),
        bias.reshape(1, 1),
    )


def solution(mesh):
    zs = mesh.shape["dp"] // 4
    xs = mesh.shape["fsdp"] // 2
    return jax.shard_map(
        functools.partial(body, zs, xs),
        mesh=mesh,
        in_specs=(
            P(("dp", "fsdp"), None),
            P("fsdp", None),
            P(("dp", "fsdp"), None),
            P("dp"),
            P(),
            P(),
        ),
        out_specs=(P(("dp", "fsdp"), None), P(("dp", "fsdp"), None), P("fsdp", None)),
        check_vma=False,
    )
```

```python
import functools

import jax
import jax.numpy as jnp
from jax import lax
from jax.experimental import pallas as pl
from jax.experimental.pallas import tpu as pltpu
from jax.sharding import PartitionSpec as P

NORM_EPS = 1e-06
MESH = pl.DeviceIdType.MESH
F32 = jnp.float32
BF16 = jnp.bfloat16
NT = (((1,), (1,)), ((), ()))
STOP = 99


def normalize(values):
    inverse = lax.rsqrt(jnp.sum(values * values, axis=-1, keepdims=True) + NORM_EPS)
    return (values * inverse, inverse)


def kernel(
    zs,
    xs,
    feats,
    wshard,
    text_emb,
    partner,
    log_scale,
    bias,
    grad_text,
    grad_feats,
    grad_weight,
    texts,
    images,
    fsplit,
    fgroup,
    fturned,
    pacc,
    pout,
    pin,
    pmid,
    pin_y,
    pback,
    proj,
    pbuf,
    wbuf,
    tpart,
    tsib,
    image_acc,
    ring_in,
    ring_out,
    yout,
    yin,
    iout,
    iin,
    grads,
    gfout,
    gfin,
    gw,
    gout,
    gsib,
    zout,
    zin,
    gyout,
    gyin,
    fin,
    send,
    recv,
):
    rows, embed = text_emb.shape
    wrows = wshard.shape[0]
    whalf = wrows // 2
    group = 2 * xs
    part_rows = rows // 2
    image_half = group * part_rows
    pair = 2 * rows
    unit = 4 * rows
    half = zs // 2
    p = lax.axis_index("dp")
    f = lax.axis_index("fsdp")
    core = lax.rem(p, 2)
    z = lax.rem(p // 2, zs)
    yh = p // (2 * zs)
    x = lax.rem(f, xs)
    yl = f // xs

    def at_z(zz):
        return (yh * (2 * zs) + zz * 2 + core, f)

    def zplus(by):
        return lax.rem(z + by + zs, zs)

    sib = (p + 1 - 2 * core, f)
    across = (p + 2 * zs * (1 - 2 * yh), f)

    def peer(k):
        dy, dx = k // xs, k % xs
        to_y = 1 - yl if dy else yl
        return to_y * xs + lax.rem(x + dx, xs)

    used = [0]
    pending = []

    def ids(count):
        first = used[0]
        used[0] += count
        return first

    def copy(src, dst, i, device):
        return pltpu.make_async_remote_copy(
            src_ref=src,
            dst_ref=dst,
            send_sem=send.at[i],
            recv_sem=recv.at[i],
            device_id=device,
            device_id_type=MESH,
        )

    def start(src, dst, i, device):
        c = copy(src, dst, i, device)
        c.start()
        pending.append(c)
        return c

    group_ks = [k for k in (1, xs - 1, xs, 2, xs + 1, 2 * xs - 1, xs + 2) if k < group]
    group_ks = list(dict.fromkeys(group_ks))
    assert len(group_ks) == group - 1

    def to_group(src, dst):
        first = ids(group)
        return [start(src(k), dst(k), first + k, (p, peer(k))) for k in group_ks]

    def wait_all(copies):
        for c in copies:
            c.wait_recv()

    dxs = list(dict.fromkeys([1, xs - 1] + list(range(2, xs - 1))))
    facing = (1 - yl) * xs + x

    def along_x(dx):
        return yl * xs + lax.rem(x + dx + xs, xs)

    def facing_x(dx):
        return (1 - yl) * xs + lax.rem(x + dx + xs, xs)

    def gather_start(buf, h):
        own = buf.at[h, f]
        cy = start(own, own, ids(1), (p, facing))
        return cy, [start(own, own, ids(1), (p, along_x(dx))) for dx in dxs]

    def gather_x_first(buf, h, copies):
        cy, cx = copies
        out = [cy]
        for dx, c in zip(dxs, cx):
            c.wait_recv()
            a = buf.at[h, along_x(-dx)]
            out.append(start(a, a, ids(1), (p, facing)))
        return out

    def gather_y_first(buf, h, copies):
        cy, cx = copies
        cy.wait_recv()
        a = buf.at[h, facing]
        return cx + [start(a, a, ids(1), (p, along_x(dx))) for dx in dxs]

    barrier = pltpu.get_barrier_semaphore()
    others = [sib, across]
    others += [at_z(zplus(k)) for k in range(1, zs)]
    others += [(p, peer(k)) for k in range(1, group)]
    for device in others:
        pl.semaphore_signal(barrier, inc=1, device_id=device, device_id_type=MESH)

    for j in range(group):
        fsplit[j] = feats[:, j * wrows : (j + 1) * wrows]
    text_unit, text_inv = normalize(text_emb[...].astype(F32))

    def chunk(q):
        y = yh if q == 0 else 1 - yh
        return pl.ds(pl.multiple_of(core * pair + y * rows, 16), rows)

    texts[z, chunk(0)] = text_unit.astype(BF16)
    fgroup[f] = fsplit[f]
    for h in range(2):
        for j in range(group):
            lane = j * rows + h * part_rows
            pbuf[h, :, j * part_rows : (j + 1) * part_rows] = partner[:, lane : lane + part_rows]
    image_acc[...] = jnp.zeros_like(image_acc)
    pl.semaphore_wait(barrier, len(others))

    fcopies = to_group(lambda k: fsplit.at[peer(k)], lambda k: fgroup.at[f])

    own_text = texts.at[z, chunk(0)]
    ty = start(own_text, own_text, ids(1), across)
    ring = {}
    text_sib = {}

    def ring_send(way, s, q):
        u = zplus(-way * s)
        a = texts.at[u, chunk(q)]
        ring[way, s, q] = start(a, a, ids(1), at_z(zplus(way)))

    def to_sib(by, q):
        a = texts.at[zplus(by), chunk(q)]
        text_sib.setdefault(by, []).append(start(a, a, ids(1), sib))

    def arrive(s, q):
        for way in (1, -1):
            if (way, s, q) not in ring:
                continue
            ring[way, s, q].wait_recv()
            if s < half - 2 or (s == half - 2 and q == (0 if way == 1 else 1)):
                ring_send(way, s + 1, q)
            by = -way * (s + 1)
            to_sib(half if by == -half else by, q)

    def text_ready(by):
        wait_all(text_sib[by])

    ring_send(1, 0, 0)
    ring_send(-1, 0, 0)
    to_sib(0, 0)

    wait_all(fcopies)
    pcopies = []

    def own_block(ref, h, j):
        return ref[h, pl.ds(pl.multiple_of(j * part_rows, 16), part_rows)]

    def sums_start_x():
        relay = [start(pout.at[0, facing_x(dx)], pmid.at[i], ids(1), (p, along_x(dx))) for i, dx in enumerate(dxs)]
        final = [start(pout.at[0, along_x(dx)], pin.at[0, i], ids(1), (p, along_x(dx))) for i, dx in enumerate(dxs)]
        return relay, final

    def sums_start_y():
        return [start(pout.at[1, facing_x(dx)], pin_y.at[i], ids(1), (p, facing)) for i, dx in enumerate(dxs + [0])]

    for h in range(2):
        cols = fgroup[:, h * part_rows : (h + 1) * part_rows].reshape(image_half, wrows)
        pacc[h] = jnp.dot(cols, wshard[...], preferred_element_type=F32)
        pout[h] = pacc[h].reshape(group, part_rows, embed).astype(BF16)
        pcopies.append(sums_start_y() if h else sums_start_x())
        if h == 0:
            arrive(0, 0)
    ty.wait_recv()
    ring_send(1, 0, 1)
    ring_send(-1, 0, 1)
    to_sib(0, 1)
    arrive(1, 0)
    for h in range(2):
        cols = fgroup[:, h * part_rows : (h + 1) * part_rows].reshape(image_half, wrows)
        fturned[h] = cols.T
    relay, final0 = pcopies[0]
    wait_all(relay)
    total = own_block(pacc, 0, facing)
    for i in range(len(dxs)):
        total += pmid[i].astype(F32)
    pback[0] = total.astype(BF16)
    final0.append(start(pback.at[0], pin.at[0, len(dxs)], ids(1), (p, facing)))
    arrive(0, 1)
    final1 = []
    for i, dx in enumerate(dxs):
        pcopies[1][i].wait_recv()
        pback[1 + i] = (own_block(pacc, 1, along_x(dx)) + pin_y[i].astype(F32)).astype(BF16)
        final1.append(start(pback.at[1 + i], pin.at[1, i], ids(1), (p, along_x(dx))))

    def project(h, copies):
        total = own_block(pacc, h, f)
        wait_all(copies)
        if h:
            pcopies[1][len(dxs)].wait_recv()
            total += pin_y[len(dxs)].astype(F32)
        for i in range(len(copies)):
            total += pin[h, i].astype(F32)
        proj[h] = total
        images[h, f] = normalize(total)[0].astype(BF16)
        return gather_start(images, h)

    first = project(0, final0)
    arrive(2, 0)
    second_half = project(1, final1)
    arrive(1, 1)
    icopies = [gather_x_first(images, 0, first)]
    icopies.append(gather_y_first(images, 1, second_half))
    arrive(3, 0)
    arrive(2, 1)

    scale = jnp.exp(log_scale[...])
    shift = bias[...]

    def front(u, h):
        block = texts[u]
        image_rows = images[h].reshape(image_half, embed)
        dots = lax.dot_general(block, image_rows, NT, preferred_element_type=F32)
        logits = scale * dots + shift
        r = lax.broadcasted_iota(jnp.int32, (unit, 1), 0)
        c_of = r // pair
        y_of = lax.rem(r // rows, 2)
        index = ((y_of * (2 * zs) + u * 2 + c_of) * group + f) * rows + lax.rem(r, rows)
        chance = 1.0 / (1.0 + jnp.exp(-logits))
        weight = jnp.where(pbuf[h] == index, chance - 1.0, chance).astype(BF16)
        wbuf[u, :, h * image_half : (h + 1) * image_half] = weight
        image_acc[h] += jnp.dot(weight.T, block, preferred_element_type=F32)

    def two_sides(by):
        def one(i, carry):
            front(lax.rem(z + zs + by * (2 * i - 1), zs), 0)
            return carry

        lax.fori_loop(0, 2, one, 0)

    iscopies = []

    def image_sums(h):
        iout[h] = image_acc[h].reshape(group, part_rows, embed).astype(BF16)
        iscopies.append(to_group(lambda k: iout.at[h, peer(k)], lambda k: iin.at[h, k]))

    text_ready(0)
    wait_all(icopies[0])
    front(z, 0)
    for s in range(1, half):
        if s == half - 1:
            arrive(s, 1)
        text_ready(-s)
        text_ready(s)
        two_sides(s)
    text_ready(half)
    front(zplus(half), 0)
    image_sums(0)
    wait_all(icopies[1])

    def second(u, carry):
        front(u, 1)
        return carry

    lax.fori_loop(0, zs, second, 0)
    image_sums(1)

    tpid = ids(zs)
    sib_pair = pl.ds(pl.multiple_of((1 - core) * pair, 16), pair)

    def part_copy(k):
        return copy(tpart.at[k, sib_pair], tsib.at[k], tpid + k, sib)

    def back(k, carry):
        d = half - (k + 1) // 2
        u = lax.rem(z + jnp.where(lax.rem(k, 2) == 1, d, zs - d), zs)
        image_rows = images[...].reshape(2 * image_half, embed)
        tpart[k] = jnp.dot(wbuf[u], image_rows, preferred_element_type=F32).astype(BF16)
        part_copy(k).start()
        return carry

    rsid, lsid = ids(half), ids(half)
    sum_r, sum_l = [], []

    def own_sum(k, lo, count):
        at = pl.ds(pl.multiple_of(core * pair + lo, 16), count)
        return tpart[k, at].astype(F32) + tsib[k, lo : lo + count].astype(F32)

    def sum_step(s):
        kr, kl = (0, 0) if s == 0 else (2 * s - 1, 2 * s)
        for k in range(0 if s == 0 else kr, kl + 1):
            part_copy(k).wait_recv()
        if s:
            sum_r[s - 1].wait_recv()
            sum_l[s - 1].wait_recv()
        if s == 0:
            ring_out[0, 0, :rows] = own_sum(0, 0, rows).astype(BF16)
            ring_out[1, 0, rows:] = own_sum(0, rows, rows).astype(BF16)
            a, b = pl.ds(0, rows), pl.ds(rows, rows)
        elif s == 1:
            ring_out[0, 1, :rows] = (own_sum(kr, 0, rows) + ring_in[0, 0, :rows].astype(F32)).astype(BF16)
            ring_out[0, 1, rows:] = own_sum(kr, rows, rows).astype(BF16)
            ring_out[1, 1, :rows] = own_sum(kl, 0, rows).astype(BF16)
            ring_out[1, 1, rows:] = (own_sum(kl, rows, rows) + ring_in[1, 0, rows:].astype(F32)).astype(BF16)
            a = b = pl.ds(0, pair)
        else:
            ring_out[0, s] = (own_sum(kr, 0, pair) + ring_in[0, s - 1].astype(F32)).astype(BF16)
            ring_out[1, s] = (own_sum(kl, 0, pair) + ring_in[1, s - 1].astype(F32)).astype(BF16)
            a = b = pl.ds(0, pair)
        sum_r.append(start(ring_out.at[0, s, a], ring_in.at[0, s, a], rsid + s, at_z(zplus(1))))
        sum_l.append(start(ring_out.at[1, s, b], ring_in.at[1, s, b], lsid + s, at_z(zplus(-1))))

    lax.fori_loop(0, 2, back, 0)
    sum_step(0)
    lax.fori_loop(2, zs, back, 0)


    def project_back(h):
        total = own_block(image_acc, h, f)
        wait_all(iscopies[h])
        for k in group_ks:
            total += iin[h, k].astype(F32)
        image_dir = scale * total
        image_unit, image_inv = normalize(proj[h])
        along = jnp.sum(image_unit * image_dir, axis=-1, keepdims=True)
        grads[h, f] = (image_inv * (image_dir - image_unit * along)).astype(BF16)
        return gather_start(grads, h)

    first = project_back(0)
    sum_step(1)
    second_half = project_back(1)
    gcopies = [gather_x_first(grads, 0, first)]
    gcopies.append(gather_y_first(grads, 1, second_half))
    sum_step(2)

    wait_all(gcopies[0])
    gw[...] = jnp.dot(
        fturned[0], grads[0].reshape(image_half, embed), preferred_element_type=F32
    )
    wait_all(gcopies[1])
    gw[...] += jnp.dot(
        fturned[1], grads[1].reshape(image_half, embed), preferred_element_type=F32
    )
    gout[...] = gw[...].astype(BF16)
    own_half = pl.ds(pl.multiple_of(core * whalf, 16), whalf)
    other_half = pl.ds(pl.multiple_of((1 - core) * whalf, 16), whalf)
    gs = start(gout.at[other_half], gsib, ids(1), sib)
    part = zout.shape[1]
    used_parts = whalf // part
    for j in range(used_parts, zs):
        zout[j] = jnp.zeros_like(zout[j])
    gs.wait_recv()
    zout[:used_parts] = (gw[own_half] + gsib[...].astype(F32)).astype(BF16).reshape(
        used_parts, part, embed
    )
    zid = ids(zs)
    zcopies = [
        start(zout.at[zplus(k)], zin.at[k], zid + k, at_z(zplus(k))) for k in range(1, zs)
    ]

    gfcopies = []
    for h in range(2):
        cols = lax.dot_general(
            grads[h].reshape(image_half, embed), wshard[...], NT, preferred_element_type=F32
        )
        gfout[h] = cols.astype(BF16).reshape(group, part_rows, wrows)
        gfcopies += to_group(lambda k: gfout.at[h, peer(k)], lambda k: gfin.at[h, f])
        gfin[h, f] = gfout[h, f]
    for s in range(3, half):
        sum_step(s)

    weight_sum = zout[z].astype(F32)
    for k, c in zip(range(1, zs), zcopies):
        c.wait_recv()
        weight_sum += zin[k].astype(F32)
    gyout[...] = weight_sum.astype(BF16)
    gy = start(gyout, gyin, ids(1), across)
    wait_all(gfcopies)
    for h in range(2):
        for j in range(group):
            at = (slice(h * part_rows, (h + 1) * part_rows), slice(j * wrows, (j + 1) * wrows))
            grad_feats[at] = gfin[h, j]
    gy.wait_recv()
    fin[core, z] = (gyout[...].astype(F32) + gyin[...].astype(F32)).astype(BF16)
    finid = ids(zs)
    fincopies = [
        start(fin.at[core, z], fin.at[core, z], finid + k, at_z(zplus(k))) for k in range(1, zs)
    ]

    part_copy(zs - 1).wait_recv()
    sum_r[half - 1].wait_recv()
    sum_l[half - 1].wait_recv()
    theirs = pl.ds(pl.multiple_of((1 - yh) * rows, 16), rows)
    ours = pl.ds(pl.multiple_of(yh * rows, 16), rows)

    def gathered(at, lo):
        here = pl.ds(pl.multiple_of(core * pair + lo, 16), rows)
        return (
            (tpart[zs - 1, here].astype(F32) + tsib[zs - 1, at].astype(F32))
            + (ring_in[0, half - 1, at].astype(F32) + ring_in[1, half - 1, at].astype(F32))
        )

    yout[...] = gathered(theirs, (1 - yh) * rows).astype(BF16)
    yc = start(yout, yin, ids(1), across)
    wait_all(fincopies)
    fs = start(fin.at[core], fin.at[core], ids(1), sib)
    yc.wait_recv()
    text_dir = scale * (gathered(ours, yh * rows) + yin[...].astype(F32))
    text_unit, text_inv = normalize(text_emb[...].astype(F32))
    along = jnp.sum(text_unit * text_dir, axis=-1, keepdims=True)
    grad_text[...] = text_inv * (text_dir - text_unit * along)
    fs.wait_recv()
    for c in range(2):
        grad_weight[c * whalf : (c + 1) * whalf] = (
            fin[c, :used_parts].reshape(whalf, embed)
        )

    for c in pending:
        c.wait_send()

    def part_done(k, carry):
        part_copy(k).wait_send()
        return carry

    lax.fori_loop(0, zs, part_done, 0)


SEMS = 192


def move(a, b, c, x, y, z):
    z[...] = c[...].astype(F32)
    x[...] = a[...]
    y[...] = b[...]


def body(zs, xs, feats, proj_weight, text_emb, partner, log_scale, bias):
    rows, width = feats.shape
    wrows, embed = proj_weight.shape
    group = 2 * xs
    pair, unit = 2 * rows, 4 * rows
    half = zs // 2
    whalf = wrows // 2
    part_rows = rows // 2
    image_half = group * part_rows
    part = -(-whalf // zs // 16) * 16
    vmem = pl.BlockSpec(memory_space=pltpu.VMEM)
    halves = ((2, group, part_rows, embed), BF16)
    scratch = [
        ((zs, unit, embed), BF16),
        halves,
        ((group, rows, wrows), BF16),
        ((group, rows, wrows), BF16),
        ((2, wrows, image_half), BF16),
        ((2, image_half, embed), F32),
        halves,
        ((2, group // 2, part_rows, embed), BF16),
        ((group // 2, part_rows, embed), BF16),
        ((group // 2, part_rows, embed), BF16),
        ((group // 2, part_rows, embed), BF16),
        ((2, part_rows, embed), F32),
        ((2, 1, image_half), jnp.int32),
        ((zs, unit, 2 * image_half), BF16),
        ((zs, unit, embed), BF16),
        ((zs, pair, embed), BF16),
        ((2, image_half, embed), F32),
        ((2, half, pair, embed), BF16),
        ((2, half, pair, embed), BF16),
        ((rows, embed), BF16),
        ((rows, embed), BF16),
        halves,
        halves,
        halves,
        ((2, group, part_rows, wrows), BF16),
        ((2, group, part_rows, wrows), BF16),
        ((wrows, embed), F32),
        ((wrows, embed), BF16),
        ((whalf, embed), BF16),
        ((zs, part, embed), BF16),
        ((zs, part, embed), BF16),
        ((part, embed), BF16),
        ((part, embed), BF16),
        ((2, zs, part, embed), BF16),
    ]
    shapes = (
        jax.ShapeDtypeStruct((rows, embed), F32),
        jax.ShapeDtypeStruct((rows, width), BF16),
        jax.ShapeDtypeStruct((wrows, embed), BF16),
    )
    outs = pl.pallas_call(
        functools.partial(kernel, zs, xs),
        out_shape=shapes,
        in_specs=[vmem] * 6,
        out_specs=(vmem,) * 3,
        scratch_shapes=[pltpu.VMEM(shape, kind) for shape, kind in scratch]
        + [pltpu.SemaphoreType.DMA((SEMS,)), pltpu.SemaphoreType.DMA((SEMS,))],
        compiler_params=pltpu.CompilerParams(
            collective_id=0, has_side_effects=True, vmem_limit_bytes=56 * 2**20
        ),
    )(
        feats,
        proj_weight,
        text_emb,
        partner.reshape(1, group * rows),
        log_scale.reshape(1, 1),
        bias.reshape(1, 1),
    )
    return pl.pallas_call(
        move,
        out_shape=shapes[:2] + (jax.ShapeDtypeStruct((wrows, embed), F32),),
        in_specs=[vmem] * 3,
        out_specs=(vmem,) * 3,
    )(*outs)


def solution(mesh):
    zs = mesh.shape["dp"] // 4
    xs = mesh.shape["fsdp"] // 2
    return jax.shard_map(
        functools.partial(body, zs, xs),
        mesh=mesh,
        in_specs=(
            P(("dp", "fsdp"), None),
            P("fsdp", None),
            P(("dp", "fsdp"), None),
            P("dp"),
            P(),
            P(),
        ),
        out_specs=(P(("dp", "fsdp"), None), P(("dp", "fsdp"), None), P("fsdp", None)),
        check_vma=False,
    )
```

```python
import functools

import jax
import jax.numpy as jnp
from jax import lax
from jax.experimental import pallas as pl
from jax.experimental.pallas import tpu as pltpu
from jax.sharding import PartitionSpec as P

NORM_EPS = 1e-06
MESH = pl.DeviceIdType.MESH
F32 = jnp.float32
BF16 = jnp.bfloat16
NT = (((1,), (1,)), ((), ()))
STOP = 99


def normalize(values):
    inverse = lax.rsqrt(jnp.sum(values * values, axis=-1, keepdims=True) + NORM_EPS)
    return (values * inverse, inverse)


def kernel(
    zs,
    xs,
    feats,
    wshard,
    text_emb,
    partner,
    log_scale,
    bias,
    grad_text,
    grad_feats,
    grad_weight,
    texts,
    images,
    fsplit,
    fgroup,
    fturned,
    pacc,
    pout,
    pin,
    pmid,
    pin_y,
    pback,
    proj,
    pbuf,
    wbuf,
    tpart,
    tsib,
    image_acc,
    ring_in,
    ring_out,
    yout,
    yin,
    iout,
    iin,
    grads,
    gfout,
    gfin,
    gw,
    gout,
    gsib,
    zout,
    zin,
    gyout,
    gyin,
    fin,
    send,
    recv,
):
    rows, embed = text_emb.shape
    wrows = wshard.shape[0]
    whalf = wrows // 2
    group = 2 * xs
    part_rows = rows // 2
    image_half = group * part_rows
    pair = 2 * rows
    unit = 4 * rows
    half = zs // 2
    p = lax.axis_index("dp")
    f = lax.axis_index("fsdp")
    core = lax.rem(p, 2)
    z = lax.rem(p // 2, zs)
    yh = p // (2 * zs)
    x = lax.rem(f, xs)
    yl = f // xs

    def at_z(zz):
        return (yh * (2 * zs) + zz * 2 + core, f)

    def zplus(by):
        return lax.rem(z + by + zs, zs)

    sib = (p + 1 - 2 * core, f)
    across = (p + 2 * zs * (1 - 2 * yh), f)

    def peer(k):
        dy, dx = k // xs, k % xs
        to_y = 1 - yl if dy else yl
        return to_y * xs + lax.rem(x + dx, xs)

    used = [0]
    pending = []

    def ids(count):
        first = used[0]
        used[0] += count
        return first

    def copy(src, dst, i, device):
        return pltpu.make_async_remote_copy(
            src_ref=src,
            dst_ref=dst,
            send_sem=send.at[i],
            recv_sem=recv.at[i],
            device_id=device,
            device_id_type=MESH,
        )

    def start(src, dst, i, device):
        c = copy(src, dst, i, device)
        c.start()
        pending.append(c)
        return c

    group_ks = [k for k in (1, xs - 1, xs, 2, xs + 1, 2 * xs - 1, xs + 2) if k < group]
    group_ks = list(dict.fromkeys(group_ks))
    assert len(group_ks) == group - 1

    def to_group(src, dst):
        first = ids(group)
        return [start(src(k), dst(k), first + k, (p, peer(k))) for k in group_ks]

    def wait_all(copies):
        for c in copies:
            c.wait_recv()

    dxs = list(dict.fromkeys([1, xs - 1] + list(range(2, xs - 1))))
    facing = (1 - yl) * xs + x

    def along_x(dx):
        return yl * xs + lax.rem(x + dx + xs, xs)

    def facing_x(dx):
        return (1 - yl) * xs + lax.rem(x + dx + xs, xs)

    def gather_start(buf, h):
        own = buf.at[h, f]
        cy = start(own, own, ids(1), (p, facing))
        return cy, [start(own, own, ids(1), (p, along_x(dx))) for dx in dxs]

    def gather_x_first(buf, h, copies):
        cy, cx = copies
        out = [cy]
        for dx, c in zip(dxs, cx):
            c.wait_recv()
            a = buf.at[h, along_x(-dx)]
            out.append(start(a, a, ids(1), (p, facing)))
        return out

    def gather_y_first(buf, h, copies):
        cy, cx = copies
        cy.wait_recv()
        a = buf.at[h, facing]
        return cx + [start(a, a, ids(1), (p, along_x(dx))) for dx in dxs]

    barrier = pltpu.get_barrier_semaphore()
    others = [sib, across]
    others += [at_z(zplus(k)) for k in range(1, zs)]
    others += [(p, peer(k)) for k in range(1, group)]
    for device in others:
        pl.semaphore_signal(barrier, inc=1, device_id=device, device_id_type=MESH)

    fsplit[...] = jnp.zeros_like(fsplit)
    gfout[...] = jnp.zeros_like(gfout)
    for j in range(group):
        fsplit[j, :, :wrows] = feats[:, j * wrows : (j + 1) * wrows]
    text_unit, text_inv = normalize(text_emb[...].astype(F32))

    def chunk(q):
        y = yh if q == 0 else 1 - yh
        return pl.ds(pl.multiple_of(core * pair + y * rows, 16), rows)

    texts[z, chunk(0)] = text_unit.astype(BF16)
    fgroup[f] = fsplit[f]
    for h in range(2):
        for j in range(group):
            lane = j * rows + h * part_rows
            pbuf[h, :, j * part_rows : (j + 1) * part_rows] = partner[:, lane : lane + part_rows]
    image_acc[...] = jnp.zeros_like(image_acc)
    pl.semaphore_wait(barrier, len(others))

    fcopies = to_group(lambda k: fsplit.at[peer(k)], lambda k: fgroup.at[f])

    own_text = texts.at[z, chunk(0)]
    ty = start(own_text, own_text, ids(1), across)
    ring = {}
    text_sib = {}

    def ring_send(way, s, q):
        u = zplus(-way * s)
        a = texts.at[u, chunk(q)]
        ring[way, s, q] = start(a, a, ids(1), at_z(zplus(way)))

    def to_sib(by, q):
        a = texts.at[zplus(by), chunk(q)]
        text_sib.setdefault(by, []).append(start(a, a, ids(1), sib))

    def arrive(s, q):
        for way in (1, -1):
            if (way, s, q) not in ring:
                continue
            ring[way, s, q].wait_recv()
            if s < half - 2 or (s == half - 2 and q == (0 if way == 1 else 1)):
                ring_send(way, s + 1, q)
            by = -way * (s + 1)
            to_sib(half if by == -half else by, q)

    def text_ready(by):
        wait_all(text_sib[by])

    ring_send(1, 0, 0)
    ring_send(-1, 0, 0)
    to_sib(0, 0)

    wait_all(fcopies)
    pcopies = []

    def own_block(ref, h, j):
        return ref[h, pl.ds(pl.multiple_of(j * part_rows, 16), part_rows)]

    def sums_start_x():
        relay = [start(pout.at[0, facing_x(dx)], pmid.at[i], ids(1), (p, along_x(dx))) for i, dx in enumerate(dxs)]
        final = [start(pout.at[0, along_x(dx)], pin.at[0, i], ids(1), (p, along_x(dx))) for i, dx in enumerate(dxs)]
        return relay, final

    def sums_start_y():
        return [start(pout.at[1, facing_x(dx)], pin_y.at[i], ids(1), (p, facing)) for i, dx in enumerate(dxs + [0])]

    for h in range(2):
        cols = fgroup[:, h * part_rows : (h + 1) * part_rows, :wrows].reshape(image_half, wrows)
        pacc[h] = jnp.dot(cols, wshard[...], preferred_element_type=F32)
        pout[h] = pacc[h].reshape(group, part_rows, embed).astype(BF16)
        pcopies.append(sums_start_y() if h else sums_start_x())
        if h == 0:
            arrive(0, 0)
    ty.wait_recv()
    ring_send(1, 0, 1)
    ring_send(-1, 0, 1)
    to_sib(0, 1)
    arrive(1, 0)
    for h in range(2):
        cols = fgroup[:, h * part_rows : (h + 1) * part_rows, :wrows].reshape(image_half, wrows)
        fturned[h] = cols.T
    relay, final0 = pcopies[0]
    wait_all(relay)
    total = own_block(pacc, 0, facing)
    for i in range(len(dxs)):
        total += pmid[i].astype(F32)
    pback[0] = total.astype(BF16)
    final0.append(start(pback.at[0], pin.at[0, len(dxs)], ids(1), (p, facing)))
    arrive(0, 1)
    final1 = []
    for i, dx in enumerate(dxs):
        pcopies[1][i].wait_recv()
        pback[1 + i] = (own_block(pacc, 1, along_x(dx)) + pin_y[i].astype(F32)).astype(BF16)
        final1.append(start(pback.at[1 + i], pin.at[1, i], ids(1), (p, along_x(dx))))

    def project(h, copies):
        total = own_block(pacc, h, f)
        wait_all(copies)
        if h:
            pcopies[1][len(dxs)].wait_recv()
            total += pin_y[len(dxs)].astype(F32)
        for i in range(len(copies)):
            total += pin[h, i].astype(F32)
        proj[h] = total
        images[h, f] = normalize(total)[0].astype(BF16)
        return gather_start(images, h)

    first = project(0, final0)
    arrive(2, 0)
    second_half = project(1, final1)
    arrive(1, 1)
    icopies = [gather_x_first(images, 0, first)]
    icopies.append(gather_y_first(images, 1, second_half))
    arrive(3, 0)
    arrive(2, 1)

    scale = jnp.exp(log_scale[...])
    half_scale = 0.5 * scale
    half_shift = 0.5 * bias[...]

    def weigh(u, h, block):
        image_rows = images[h].reshape(image_half, embed)
        dots = lax.dot_general(block, image_rows, NT, preferred_element_type=F32)
        r = lax.broadcasted_iota(jnp.int32, (unit, 1), 0)
        c_of = r // pair
        y_of = lax.rem(r // rows, 2)
        index = ((y_of * (2 * zs) + u * 2 + c_of) * group + f) * rows + lax.rem(r, rows)
        level = jnp.where(pbuf[h] == index, F32(-0.5), F32(0.5))
        weight = (0.5 * jnp.tanh(half_scale * dots + half_shift) + level).astype(BF16)
        wbuf[u, :, h * image_half : (h + 1) * image_half] = weight
        return weight

    def front(units, h):
        blocks = [texts[u] for u in units]
        weights = [weigh(u, h, block) for u, block in zip(units, blocks)]
        total = jnp.dot(weights[0].T, blocks[0], preferred_element_type=F32)
        for weight, block in zip(weights[1:], blocks[1:]):
            total += jnp.dot(weight.T, block, preferred_element_type=F32)
        image_acc[h] += total

    iscopies = []

    def image_sums(h):
        iout[h] = image_acc[h].reshape(group, part_rows, embed).astype(BF16)
        iscopies.append(to_group(lambda k: iout.at[h, peer(k)], lambda k: iin.at[h, k]))

    text_ready(0)
    wait_all(icopies[0])
    front([z], 0)
    for s in range(1, half):
        if s == half - 1:
            arrive(s, 1)
        text_ready(-s)
        text_ready(s)
        front([zplus(-s), zplus(s)], 0)
    text_ready(half)
    front([zplus(half)], 0)
    image_sums(0)
    wait_all(icopies[1])

    def second(i, carry):
        front([2 * i, 2 * i + 1], 1)
        return carry

    lax.fori_loop(0, zs // 2, second, 0)
    image_sums(1)

    tpid = ids(zs)
    sib_pair = pl.ds(pl.multiple_of((1 - core) * pair, 16), pair)

    def part_copy(k):
        return copy(tpart.at[k, sib_pair], tsib.at[k], tpid + k, sib)

    def back(k, carry):
        d = half - (k + 1) // 2
        u = lax.rem(z + jnp.where(lax.rem(k, 2) == 1, d, zs - d), zs)
        image_rows = images[...].reshape(2 * image_half, embed)
        tpart[k] = jnp.dot(wbuf[u], image_rows, preferred_element_type=F32).astype(BF16)
        part_copy(k).start()
        return carry

    rsid, lsid = ids(half), ids(half)
    sum_r, sum_l = [], []

    def own_sum(k, lo, count):
        at = pl.ds(pl.multiple_of(core * pair + lo, 16), count)
        return tpart[k, at].astype(F32) + tsib[k, lo : lo + count].astype(F32)

    def sum_step(s):
        kr, kl = (0, 0) if s == 0 else (2 * s - 1, 2 * s)
        for k in range(0 if s == 0 else kr, kl + 1):
            part_copy(k).wait_recv()
        if s:
            sum_r[s - 1].wait_recv()
            sum_l[s - 1].wait_recv()
        if s == 0:
            ring_out[0, 0, :rows] = own_sum(0, 0, rows).astype(BF16)
            ring_out[1, 0, rows:] = own_sum(0, rows, rows).astype(BF16)
            a, b = pl.ds(0, rows), pl.ds(rows, rows)
        elif s == 1:
            ring_out[0, 1, :rows] = (own_sum(kr, 0, rows) + ring_in[0, 0, :rows].astype(F32)).astype(BF16)
            ring_out[0, 1, rows:] = own_sum(kr, rows, rows).astype(BF16)
            ring_out[1, 1, :rows] = own_sum(kl, 0, rows).astype(BF16)
            ring_out[1, 1, rows:] = (own_sum(kl, rows, rows) + ring_in[1, 0, rows:].astype(F32)).astype(BF16)
            a = b = pl.ds(0, pair)
        else:
            ring_out[0, s] = (own_sum(kr, 0, pair) + ring_in[0, s - 1].astype(F32)).astype(BF16)
            ring_out[1, s] = (own_sum(kl, 0, pair) + ring_in[1, s - 1].astype(F32)).astype(BF16)
            a = b = pl.ds(0, pair)
        sum_r.append(start(ring_out.at[0, s, a], ring_in.at[0, s, a], rsid + s, at_z(zplus(1))))
        sum_l.append(start(ring_out.at[1, s, b], ring_in.at[1, s, b], lsid + s, at_z(zplus(-1))))

    lax.fori_loop(0, 2, back, 0)
    sum_step(0)
    lax.fori_loop(2, zs, back, 0, unroll=2)


    def project_back(h):
        total = own_block(image_acc, h, f)
        wait_all(iscopies[h])
        for k in group_ks:
            total += iin[h, k].astype(F32)
        image_dir = scale * total
        image_unit, image_inv = normalize(proj[h])
        along = jnp.sum(image_unit * image_dir, axis=-1, keepdims=True)
        grads[h, f] = (image_inv * (image_dir - image_unit * along)).astype(BF16)
        return gather_start(grads, h)

    first = project_back(0)
    sum_step(1)
    second_half = project_back(1)
    gcopies = [gather_x_first(grads, 0, first)]
    gcopies.append(gather_y_first(grads, 1, second_half))
    sum_step(2)

    own_half = pl.ds(pl.multiple_of(core * whalf, 16), whalf)
    other_half = pl.ds(pl.multiple_of((1 - core) * whalf, 16), whalf)
    part = zout.shape[1]
    used_parts = whalf // part
    for j in range(used_parts, zs):
        zout[j] = jnp.zeros_like(zout[j])
    middle = (embed // 128 + 1) // 2 * 128
    cuts = [slice(0, middle), slice(middle, embed)]

    def weight_part(h, at, cut):
        some = grads[h, :, :, cut].reshape(image_half, cut.stop - cut.start)
        return jnp.dot(fturned[h, at], some, preferred_element_type=F32)

    wait_all(gcopies[0])
    for cut in cuts:
        gw[0, :, cut] = weight_part(0, other_half, cut)
        gw[1, :, cut] = weight_part(0, own_half, cut)
    wait_all(gcopies[1])
    gs = []
    for cut in cuts:
        gout[:, cut] = (gw[0, :, cut] + weight_part(1, other_half, cut)).astype(BF16)
        gs.append(start(gout.at[:, cut], gsib.at[:, cut], ids(1), sib))
        gw[1, :, cut] += weight_part(1, own_half, cut)
    zcopies = []
    for cut, c in zip(cuts, gs):
        c.wait_recv()
        total = (gw[1, :, cut] + gsib[:, cut].astype(F32)).astype(BF16)
        zout[:used_parts, :, cut] = total.reshape(used_parts, part, cut.stop - cut.start)
        zcopies.append(
            [
                start(zout.at[zplus(k), :, cut], zin.at[k, :, cut], ids(1), at_z(zplus(k)))
                for k in range(1, zs)
            ]
        )

    gfcopies = []
    for h in range(2):
        cols = lax.dot_general(
            grads[h].reshape(image_half, embed), wshard[...], NT, preferred_element_type=F32
        )
        gfout[h, :, :, :wrows] = cols.astype(BF16).reshape(group, part_rows, wrows)
        gfcopies += to_group(lambda k: gfout.at[h, peer(k)], lambda k: gfin.at[h, f])
        gfin[h, f] = gfout[h, f]
    for s in range(3, half):
        sum_step(s)

    gy = []
    for cut, copies in zip(cuts, zcopies):
        weight_sum = zout[z, :, cut].astype(F32)
        for k, c in zip(range(1, zs), copies):
            c.wait_recv()
            weight_sum += zin[k, :, cut].astype(F32)
        gyout[:, cut] = weight_sum.astype(BF16)
        gy.append(start(gyout.at[:, cut], gyin.at[:, cut], ids(1), across))
    fincopies = []
    for cut, c in zip(cuts, gy):
        c.wait_recv()
        fin[core, z, :, cut] = (
            gyout[:, cut].astype(F32) + gyin[:, cut].astype(F32)
        ).astype(BF16)
        own = fin.at[core, z, :, cut]
        fincopies.append([start(own, own, ids(1), at_z(zplus(k))) for k in range(1, zs)])
    wait_all(gfcopies)
    for h in range(2):
        for j in range(group):
            at = (slice(h * part_rows, (h + 1) * part_rows), slice(j * wrows, (j + 1) * wrows))
            grad_feats[at] = gfin[h, j, :, :wrows]

    part_copy(zs - 1).wait_recv()
    sum_r[half - 1].wait_recv()
    sum_l[half - 1].wait_recv()
    theirs = pl.ds(pl.multiple_of((1 - yh) * rows, 16), rows)
    ours = pl.ds(pl.multiple_of(yh * rows, 16), rows)

    def gathered(at, lo):
        here = pl.ds(pl.multiple_of(core * pair + lo, 16), rows)
        return (
            (tpart[zs - 1, here].astype(F32) + tsib[zs - 1, at].astype(F32))
            + (ring_in[0, half - 1, at].astype(F32) + ring_in[1, half - 1, at].astype(F32))
        )

    yout[...] = gathered(theirs, (1 - yh) * rows).astype(BF16)
    yc = start(yout, yin, ids(1), across)
    fs = []
    for cut, copies in zip(cuts, fincopies):
        wait_all(copies)
        own = fin.at[core, :, :, cut]
        fs.append(start(own, own, ids(1), sib))
    yc.wait_recv()
    text_dir = scale * (gathered(ours, yh * rows) + yin[...].astype(F32))
    text_unit, text_inv = normalize(text_emb[...].astype(F32))
    along = jnp.sum(text_unit * text_dir, axis=-1, keepdims=True)
    grad_text[...] = text_inv * (text_dir - text_unit * along)
    wait_all(fs)
    for c in range(2):
        grad_weight[c * whalf : (c + 1) * whalf] = (
            fin[c, :used_parts].reshape(whalf, embed)
        )

    for c in pending:
        c.wait_send()

    def part_done(k, carry):
        part_copy(k).wait_send()
        return carry

    lax.fori_loop(0, zs, part_done, 0)


SEMS = 224


def move(a, b, c, x, y, z):
    z[...] = c[...].astype(F32)
    x[...] = a[...]
    y[...] = b[...]


def body(zs, xs, feats, proj_weight, text_emb, partner, log_scale, bias):
    rows, width = feats.shape
    wrows, embed = proj_weight.shape
    group = 2 * xs
    pair, unit = 2 * rows, 4 * rows
    half = zs // 2
    whalf = wrows // 2
    part_rows = rows // 2
    image_half = group * part_rows
    lanes = -(-wrows // 128) * 128
    part = -(-whalf // zs // 16) * 16
    vmem = pl.BlockSpec(memory_space=pltpu.VMEM)
    halves = ((2, group, part_rows, embed), BF16)
    scratch = [
        ((zs, unit, embed), BF16),
        halves,
        ((group, rows, lanes), BF16),
        ((group, rows, lanes), BF16),
        ((2, wrows, image_half), BF16),
        ((2, image_half, embed), F32),
        halves,
        ((2, group // 2, part_rows, embed), BF16),
        ((group // 2, part_rows, embed), BF16),
        ((group // 2, part_rows, embed), BF16),
        ((group // 2, part_rows, embed), BF16),
        ((2, part_rows, embed), F32),
        ((2, 1, image_half), jnp.int32),
        ((zs, unit, 2 * image_half), BF16),
        ((zs, unit, embed), BF16),
        ((zs, pair, embed), BF16),
        ((2, image_half, embed), F32),
        ((2, half, pair, embed), BF16),
        ((2, half, pair, embed), BF16),
        ((rows, embed), BF16),
        ((rows, embed), BF16),
        halves,
        halves,
        halves,
        ((2, group, part_rows, lanes), BF16),
        ((2, group, part_rows, lanes), BF16),
        ((2, whalf, embed), F32),
        ((whalf, embed), BF16),
        ((whalf, embed), BF16),
        ((zs, part, embed), BF16),
        ((zs, part, embed), BF16),
        ((part, embed), BF16),
        ((part, embed), BF16),
        ((2, zs, part, embed), BF16),
    ]
    shapes = (
        jax.ShapeDtypeStruct((rows, embed), F32),
        jax.ShapeDtypeStruct((rows, width), BF16),
        jax.ShapeDtypeStruct((wrows, embed), BF16),
    )
    outs = pl.pallas_call(
        functools.partial(kernel, zs, xs),
        out_shape=shapes,
        in_specs=[vmem] * 6,
        out_specs=(vmem,) * 3,
        scratch_shapes=[pltpu.VMEM(shape, kind) for shape, kind in scratch]
        + [pltpu.SemaphoreType.DMA((SEMS,)), pltpu.SemaphoreType.DMA((SEMS,))],
        compiler_params=pltpu.CompilerParams(
            collective_id=0, has_side_effects=True, vmem_limit_bytes=56 * 2**20
        ),
    )(
        feats,
        proj_weight,
        text_emb,
        partner.reshape(1, group * rows),
        log_scale.reshape(1, 1),
        bias.reshape(1, 1),
    )
    return pl.pallas_call(
        move,
        out_shape=shapes[:2] + (jax.ShapeDtypeStruct((wrows, embed), F32),),
        in_specs=[vmem] * 3,
        out_specs=(vmem,) * 3,
    )(*outs)


def solution(mesh):
    zs = mesh.shape["dp"] // 4
    xs = mesh.shape["fsdp"] // 2
    return jax.shard_map(
        functools.partial(body, zs, xs),
        mesh=mesh,
        in_specs=(
            P(("dp", "fsdp"), None),
            P("fsdp", None),
            P(("dp", "fsdp"), None),
            P("dp"),
            P(),
            P(),
        ),
        out_specs=(P(("dp", "fsdp"), None), P(("dp", "fsdp"), None), P("fsdp", None)),
        check_vma=False,
    )
```

```python
import functools

import jax
import jax.numpy as jnp
from jax import lax
from jax.experimental import pallas as pl
from jax.experimental.pallas import tpu as pltpu
from jax.sharding import PartitionSpec as P

NORM_EPS = 1e-06
MESH = pl.DeviceIdType.MESH
F32 = jnp.float32
BF16 = jnp.bfloat16
NT = (((1,), (1,)), ((), ()))
STOP = 99


def normalize(values):
    inverse = lax.rsqrt(jnp.sum(values * values, axis=-1, keepdims=True) + NORM_EPS)
    return (values * inverse, inverse)


def kernel(
    zs,
    xs,
    feats_in,
    wshard_in,
    text_in,
    partner,
    log_scale,
    bias,
    grad_text_out,
    grad_feats_out,
    grad_weight_out,
    feats,
    wshard,
    text_emb,
    grad_text,
    grad_feats,
    grad_weight,
    texts,
    images,
    fsplit,
    fgroup,
    fturned,
    pacc,
    pout,
    pin,
    pmid,
    pin_y,
    pback,
    proj,
    pbuf,
    wbuf,
    tpart,
    tsib,
    image_acc,
    ring_in,
    ring_out,
    yout,
    yin,
    iout,
    iin,
    grads,
    gfout,
    gfin,
    gw,
    gout,
    gsib,
    zout,
    zin,
    gyout,
    gyin,
    fin,
    send,
    recv,
    local,
):
    rows, embed = text_emb.shape
    wrows = wshard.shape[0]
    whalf = wrows // 2
    group = 2 * xs
    part_rows = rows // 2
    image_half = group * part_rows
    pair = 2 * rows
    unit = 4 * rows
    half = zs // 2
    p = lax.axis_index("dp")
    f = lax.axis_index("fsdp")
    core = lax.rem(p, 2)
    z = lax.rem(p // 2, zs)
    yh = p // (2 * zs)
    x = lax.rem(f, xs)
    yl = f // xs

    def at_z(zz):
        return (yh * (2 * zs) + zz * 2 + core, f)

    def zplus(by):
        return lax.rem(z + by + zs, zs)

    sib = (p + 1 - 2 * core, f)
    across = (p + 2 * zs * (1 - 2 * yh), f)

    def peer(k):
        dy, dx = k // xs, k % xs
        to_y = 1 - yl if dy else yl
        return to_y * xs + lax.rem(x + dx, xs)

    used = [0]
    pending = []

    def ids(count):
        first = used[0]
        used[0] += count
        return first

    def copy(src, dst, i, device):
        return pltpu.make_async_remote_copy(
            src_ref=src,
            dst_ref=dst,
            send_sem=send.at[i],
            recv_sem=recv.at[i],
            device_id=device,
            device_id_type=MESH,
        )

    def start(src, dst, i, device):
        c = copy(src, dst, i, device)
        c.start()
        pending.append(c)
        return c

    group_ks = [k for k in (1, xs - 1, xs, 2, xs + 1, 2 * xs - 1, xs + 2) if k < group]
    group_ks = list(dict.fromkeys(group_ks))
    assert len(group_ks) == group - 1

    def to_group(src, dst):
        first = ids(group)
        return [start(src(k), dst(k), first + k, (p, peer(k))) for k in group_ks]

    def wait_all(copies):
        for c in copies:
            c.wait_recv()

    dxs = list(dict.fromkeys([1, xs - 1] + list(range(2, xs - 1))))
    facing = (1 - yl) * xs + x

    def along_x(dx):
        return yl * xs + lax.rem(x + dx + xs, xs)

    def facing_x(dx):
        return (1 - yl) * xs + lax.rem(x + dx + xs, xs)

    def gather_start(buf, h):
        own = buf.at[h, f]
        cy = start(own, own, ids(1), (p, facing))
        return cy, [start(own, own, ids(1), (p, along_x(dx))) for dx in dxs]

    def gather_x_first(buf, h, copies):
        cy, cx = copies
        out = [cy]
        for dx, c in zip(dxs, cx):
            c.wait_recv()
            a = buf.at[h, along_x(-dx)]
            out.append(start(a, a, ids(1), (p, facing)))
        return out

    def gather_y_first(buf, h, copies):
        cy, cx = copies
        cy.wait_recv()
        a = buf.at[h, facing]
        return cx + [start(a, a, ids(1), (p, along_x(dx))) for dx in dxs]

    feats_load = pltpu.make_async_copy(feats_in, feats, local.at[0])
    text_load = pltpu.make_async_copy(text_in, text_emb, local.at[1])
    weight_load = pltpu.make_async_copy(wshard_in, wshard, local.at[2])
    for c in (feats_load, text_load, weight_load):
        c.start()

    barrier = pltpu.get_barrier_semaphore()
    others = [sib, across]
    others += [at_z(zplus(k)) for k in range(1, zs)]
    others += [(p, peer(k)) for k in range(1, group)]
    for device in others:
        pl.semaphore_signal(barrier, inc=1, device_id=device, device_id_type=MESH)

    feats_load.wait()
    fsplit[...] = jnp.zeros_like(fsplit)
    for j in range(group):
        fsplit[j, :, :wrows] = feats[:, j * wrows : (j + 1) * wrows]
    pl.semaphore_wait(barrier, len(others))
    fcopies = to_group(lambda k: fsplit.at[peer(k)], lambda k: fgroup.at[f])

    text_load.wait()
    text_unit, text_inv = normalize(text_emb[...].astype(F32))

    def chunk(q):
        y = yh if q == 0 else 1 - yh
        return pl.ds(pl.multiple_of(core * pair + y * rows, 16), rows)

    texts[z, chunk(0)] = text_unit.astype(BF16)
    own_text = texts.at[z, chunk(0)]
    ty = start(own_text, own_text, ids(1), across)
    ring = {}
    text_sib = {}

    def ring_send(way, s, q):
        u = zplus(-way * s)
        a = texts.at[u, chunk(q)]
        ring[way, s, q] = start(a, a, ids(1), at_z(zplus(way)))

    def to_sib(by, q):
        a = texts.at[zplus(by), chunk(q)]
        text_sib.setdefault(by, []).append(start(a, a, ids(1), sib))

    def arrive(s, q):
        for way in (1, -1):
            if (way, s, q) not in ring:
                continue
            ring[way, s, q].wait_recv()
            if s < half - 2 or (s == half - 2 and q == (0 if way == 1 else 1)):
                ring_send(way, s + 1, q)
            by = -way * (s + 1)
            to_sib(half if by == -half else by, q)

    def text_ready(by):
        wait_all(text_sib[by])

    ring_send(1, 0, 0)
    ring_send(-1, 0, 0)
    to_sib(0, 0)

    fgroup[f] = fsplit[f]
    gfout[...] = jnp.zeros_like(gfout)
    for h in range(2):
        for j in range(group):
            lane = j * rows + h * part_rows
            pbuf[h, :, j * part_rows : (j + 1) * part_rows] = partner[:, lane : lane + part_rows]
    image_acc[...] = jnp.zeros_like(image_acc)

    weight_load.wait()
    wait_all(fcopies)
    pcopies = []

    def own_block(ref, h, j):
        return ref[h, pl.ds(pl.multiple_of(j * part_rows, 16), part_rows)]

    def sums_start_x():
        relay = [start(pout.at[0, facing_x(dx)], pmid.at[i], ids(1), (p, along_x(dx))) for i, dx in enumerate(dxs)]
        final = [start(pout.at[0, along_x(dx)], pin.at[0, i], ids(1), (p, along_x(dx))) for i, dx in enumerate(dxs)]
        return relay, final

    def sums_start_y():
        return [start(pout.at[1, facing_x(dx)], pin_y.at[i], ids(1), (p, facing)) for i, dx in enumerate(dxs + [0])]

    for h in range(2):
        cols = fgroup[:, h * part_rows : (h + 1) * part_rows, :wrows].reshape(image_half, wrows)
        pacc[h] = jnp.dot(cols, wshard[...], preferred_element_type=F32)
        pout[h] = pacc[h].reshape(group, part_rows, embed).astype(BF16)
        pcopies.append(sums_start_y() if h else sums_start_x())
        if h == 0:
            arrive(0, 0)
    ty.wait_recv()
    ring_send(1, 0, 1)
    ring_send(-1, 0, 1)
    to_sib(0, 1)
    arrive(1, 0)
    for h in range(2):
        cols = fgroup[:, h * part_rows : (h + 1) * part_rows, :wrows].reshape(image_half, wrows)
        fturned[h] = cols.T
    relay, final0 = pcopies[0]
    wait_all(relay)
    total = own_block(pacc, 0, facing)
    for i in range(len(dxs)):
        total += pmid[i].astype(F32)
    pback[0] = total.astype(BF16)
    final0.append(start(pback.at[0], pin.at[0, len(dxs)], ids(1), (p, facing)))
    arrive(0, 1)
    final1 = []
    for i, dx in enumerate(dxs):
        pcopies[1][i].wait_recv()
        pback[1 + i] = (own_block(pacc, 1, along_x(dx)) + pin_y[i].astype(F32)).astype(BF16)
        final1.append(start(pback.at[1 + i], pin.at[1, i], ids(1), (p, along_x(dx))))

    def project(h, copies):
        total = own_block(pacc, h, f)
        wait_all(copies)
        if h:
            pcopies[1][len(dxs)].wait_recv()
            total += pin_y[len(dxs)].astype(F32)
        for i in range(len(copies)):
            total += pin[h, i].astype(F32)
        proj[h] = total
        images[h, f] = normalize(total)[0].astype(BF16)
        return gather_start(images, h)

    first = project(0, final0)
    arrive(2, 0)
    second_half = project(1, final1)
    arrive(1, 1)
    icopies = [gather_x_first(images, 0, first)]
    icopies.append(gather_y_first(images, 1, second_half))
    arrive(3, 0)
    arrive(2, 1)

    scale = jnp.exp(log_scale[...])
    half_scale = 0.5 * scale
    half_shift = 0.5 * bias[...]

    def weigh(u, h, block):
        image_rows = images[h].reshape(image_half, embed)
        dots = lax.dot_general(block, image_rows, NT, preferred_element_type=F32)
        r = lax.broadcasted_iota(jnp.int32, (unit, 1), 0)
        c_of = r // pair
        y_of = lax.rem(r // rows, 2)
        index = ((y_of * (2 * zs) + u * 2 + c_of) * group + f) * rows + lax.rem(r, rows)
        level = jnp.where(pbuf[h] == index, F32(-0.5), F32(0.5))
        weight = (0.5 * jnp.tanh(half_scale * dots + half_shift) + level).astype(BF16)
        wbuf[u, :, h * image_half : (h + 1) * image_half] = weight
        return weight

    def front(units, h):
        blocks = [texts[u] for u in units]
        weights = [weigh(u, h, block) for u, block in zip(units, blocks)]
        total = jnp.dot(weights[0].T, blocks[0], preferred_element_type=F32)
        for weight, block in zip(weights[1:], blocks[1:]):
            total += jnp.dot(weight.T, block, preferred_element_type=F32)
        image_acc[h] += total

    iscopies = []

    def image_sums(h):
        iout[h] = image_acc[h].reshape(group, part_rows, embed).astype(BF16)
        iscopies.append(to_group(lambda k: iout.at[h, peer(k)], lambda k: iin.at[h, k]))

    text_ready(0)
    wait_all(icopies[0])
    front([z], 0)
    for s in range(1, half):
        if s == half - 1:
            arrive(s, 1)
        text_ready(-s)
        text_ready(s)
        front([zplus(-s), zplus(s)], 0)
    text_ready(half)
    front([zplus(half)], 0)
    image_sums(0)
    wait_all(icopies[1])

    def second(i, carry):
        front([2 * i, 2 * i + 1], 1)
        return carry

    lax.fori_loop(0, zs // 2, second, 0)
    image_sums(1)

    tpid = ids(zs)
    sib_pair = pl.ds(pl.multiple_of((1 - core) * pair, 16), pair)

    def part_copy(k):
        return copy(tpart.at[k, sib_pair], tsib.at[k], tpid + k, sib)

    def back(k, carry):
        d = half - (k + 1) // 2
        u = lax.rem(z + jnp.where(lax.rem(k, 2) == 1, d, zs - d), zs)
        image_rows = images[...].reshape(2 * image_half, embed)
        tpart[k] = jnp.dot(wbuf[u], image_rows, preferred_element_type=F32).astype(BF16)
        part_copy(k).start()
        return carry

    rsid, lsid = ids(half), ids(half)
    sum_r, sum_l = [], []

    def own_sum(k, lo, count):
        at = pl.ds(pl.multiple_of(core * pair + lo, 16), count)
        return tpart[k, at].astype(F32) + tsib[k, lo : lo + count].astype(F32)

    def sum_step(s):
        kr, kl = (0, 0) if s == 0 else (2 * s - 1, 2 * s)
        for k in range(0 if s == 0 else kr, kl + 1):
            part_copy(k).wait_recv()
        if s:
            sum_r[s - 1].wait_recv()
            sum_l[s - 1].wait_recv()
        if s == 0:
            ring_out[0, 0, :rows] = own_sum(0, 0, rows).astype(BF16)
            ring_out[1, 0, rows:] = own_sum(0, rows, rows).astype(BF16)
            a, b = pl.ds(0, rows), pl.ds(rows, rows)
        elif s == 1:
            ring_out[0, 1, :rows] = (own_sum(kr, 0, rows) + ring_in[0, 0, :rows].astype(F32)).astype(BF16)
            ring_out[0, 1, rows:] = own_sum(kr, rows, rows).astype(BF16)
            ring_out[1, 1, :rows] = own_sum(kl, 0, rows).astype(BF16)
            ring_out[1, 1, rows:] = (own_sum(kl, rows, rows) + ring_in[1, 0, rows:].astype(F32)).astype(BF16)
            a = b = pl.ds(0, pair)
        else:
            ring_out[0, s] = (own_sum(kr, 0, pair) + ring_in[0, s - 1].astype(F32)).astype(BF16)
            ring_out[1, s] = (own_sum(kl, 0, pair) + ring_in[1, s - 1].astype(F32)).astype(BF16)
            a = b = pl.ds(0, pair)
        sum_r.append(start(ring_out.at[0, s, a], ring_in.at[0, s, a], rsid + s, at_z(zplus(1))))
        sum_l.append(start(ring_out.at[1, s, b], ring_in.at[1, s, b], lsid + s, at_z(zplus(-1))))

    lax.fori_loop(0, 2, back, 0)
    sum_step(0)
    lax.fori_loop(2, zs, back, 0, unroll=2)


    def project_back(h):
        total = own_block(image_acc, h, f)
        wait_all(iscopies[h])
        for k in group_ks:
            total += iin[h, k].astype(F32)
        image_dir = scale * total
        image_unit, image_inv = normalize(proj[h])
        along = jnp.sum(image_unit * image_dir, axis=-1, keepdims=True)
        grads[h, f] = (image_inv * (image_dir - image_unit * along)).astype(BF16)
        return gather_start(grads, h)

    first = project_back(0)
    sum_step(1)
    second_half = project_back(1)
    gcopies = [gather_x_first(grads, 0, first)]
    gcopies.append(gather_y_first(grads, 1, second_half))
    sum_step(2)

    own_half = pl.ds(pl.multiple_of(core * whalf, 16), whalf)
    other_half = pl.ds(pl.multiple_of((1 - core) * whalf, 16), whalf)
    part = zout.shape[1]
    used_parts = whalf // part
    for j in range(used_parts, zs):
        zout[j] = jnp.zeros_like(zout[j])
    middle = (embed // 128 + 1) // 2 * 128
    cuts = [slice(0, middle), slice(middle, embed)]

    def weight_part(h, at, cut):
        some = grads[h, :, :, cut].reshape(image_half, cut.stop - cut.start)
        return jnp.dot(fturned[h, at], some, preferred_element_type=F32)

    wait_all(gcopies[0])
    for cut in cuts:
        gw[0, :, cut] = weight_part(0, other_half, cut)
        gw[1, :, cut] = weight_part(0, own_half, cut)
    wait_all(gcopies[1])
    gs = []
    for cut in cuts:
        gout[:, cut] = (gw[0, :, cut] + weight_part(1, other_half, cut)).astype(BF16)
        gs.append(start(gout.at[:, cut], gsib.at[:, cut], ids(1), sib))
        gw[1, :, cut] += weight_part(1, own_half, cut)
    zcopies = []
    for cut, c in zip(cuts, gs):
        c.wait_recv()
        total = (gw[1, :, cut] + gsib[:, cut].astype(F32)).astype(BF16)
        zout[:used_parts, :, cut] = total.reshape(used_parts, part, cut.stop - cut.start)
        zcopies.append(
            [
                start(zout.at[zplus(k), :, cut], zin.at[k, :, cut], ids(1), at_z(zplus(k)))
                for k in range(1, zs)
            ]
        )

    gfcopies = []
    for h in range(2):
        cols = lax.dot_general(
            grads[h].reshape(image_half, embed), wshard[...], NT, preferred_element_type=F32
        )
        gfout[h, :, :, :wrows] = cols.astype(BF16).reshape(group, part_rows, wrows)
        gfcopies += to_group(lambda k: gfout.at[h, peer(k)], lambda k: gfin.at[h, f])
        gfin[h, f] = gfout[h, f]
    for s in range(3, half):
        sum_step(s)

    gy = []
    for cut, copies in zip(cuts, zcopies):
        weight_sum = zout[z, :, cut].astype(F32)
        for k, c in zip(range(1, zs), copies):
            c.wait_recv()
            weight_sum += zin[k, :, cut].astype(F32)
        gyout[:, cut] = weight_sum.astype(BF16)
        gy.append(start(gyout.at[:, cut], gyin.at[:, cut], ids(1), across))
    fincopies = []
    for cut, c in zip(cuts, gy):
        c.wait_recv()
        fin[core, z, :, cut] = (
            gyout[:, cut].astype(F32) + gyin[:, cut].astype(F32)
        ).astype(BF16)
        own = fin.at[core, z, :, cut]
        fincopies.append([start(own, own, ids(1), at_z(zplus(k))) for k in range(1, zs)])
    wait_all(gfcopies)
    for h in range(2):
        for j in range(group):
            at = (slice(h * part_rows, (h + 1) * part_rows), slice(j * wrows, (j + 1) * wrows))
            grad_feats[at] = gfin[h, j, :, :wrows]
    feats_store = pltpu.make_async_copy(grad_feats, grad_feats_out, local.at[0])
    feats_store.start()

    part_copy(zs - 1).wait_recv()
    sum_r[half - 1].wait_recv()
    sum_l[half - 1].wait_recv()
    theirs = pl.ds(pl.multiple_of((1 - yh) * rows, 16), rows)
    ours = pl.ds(pl.multiple_of(yh * rows, 16), rows)

    def gathered(at, lo):
        here = pl.ds(pl.multiple_of(core * pair + lo, 16), rows)
        return (
            (tpart[zs - 1, here].astype(F32) + tsib[zs - 1, at].astype(F32))
            + (ring_in[0, half - 1, at].astype(F32) + ring_in[1, half - 1, at].astype(F32))
        )

    yout[...] = gathered(theirs, (1 - yh) * rows).astype(BF16)
    yc = start(yout, yin, ids(1), across)
    fs = []
    for cut, copies in zip(cuts, fincopies):
        wait_all(copies)
        own = fin.at[core, :, :, cut]
        fs.append(start(own, own, ids(1), sib))
    yc.wait_recv()
    text_dir = scale * (gathered(ours, yh * rows) + yin[...].astype(F32))
    text_unit, text_inv = normalize(text_emb[...].astype(F32))
    along = jnp.sum(text_unit * text_dir, axis=-1, keepdims=True)
    grad_text[...] = text_inv * (text_dir - text_unit * along)
    text_store = pltpu.make_async_copy(grad_text, grad_text_out, local.at[1])
    text_store.start()
    wait_all(fs)
    for c in range(2):
        grad_weight[c * whalf : (c + 1) * whalf] = (
            fin[c, :used_parts].reshape(whalf, embed)
        )
    weight_store = pltpu.make_async_copy(grad_weight, grad_weight_out, local.at[2])
    weight_store.start()

    for c in pending:
        c.wait_send()

    def part_done(k, carry):
        part_copy(k).wait_send()
        return carry

    lax.fori_loop(0, zs, part_done, 0)
    feats_store.wait()
    text_store.wait()
    weight_store.wait()


SEMS = 224


def move(a, b, c, x, y, z):
    z[...] = c[...].astype(F32)
    x[...] = a[...]
    y[...] = b[...]


def body(zs, xs, feats, proj_weight, text_emb, partner, log_scale, bias):
    rows, width = feats.shape
    wrows, embed = proj_weight.shape
    group = 2 * xs
    pair, unit = 2 * rows, 4 * rows
    half = zs // 2
    whalf = wrows // 2
    part_rows = rows // 2
    image_half = group * part_rows
    lanes = -(-wrows // 128) * 128
    part = -(-whalf // zs // 16) * 16
    vmem = pl.BlockSpec(memory_space=pltpu.VMEM)
    anywhere = pl.BlockSpec(memory_space=pl.ANY)
    halves = ((2, group, part_rows, embed), BF16)
    scratch = [
        ((rows, width), BF16),
        ((wrows, embed), BF16),
        ((rows, embed), BF16),
        ((rows, embed), F32),
        ((rows, width), BF16),
        ((wrows, embed), BF16),
        ((zs, unit, embed), BF16),
        halves,
        ((group, rows, lanes), BF16),
        ((group, rows, lanes), BF16),
        ((2, wrows, image_half), BF16),
        ((2, image_half, embed), F32),
        halves,
        ((2, group // 2, part_rows, embed), BF16),
        ((group // 2, part_rows, embed), BF16),
        ((group // 2, part_rows, embed), BF16),
        ((group // 2, part_rows, embed), BF16),
        ((2, part_rows, embed), F32),
        ((2, 1, image_half), jnp.int32),
        ((zs, unit, 2 * image_half), BF16),
        ((zs, unit, embed), BF16),
        ((zs, pair, embed), BF16),
        ((2, image_half, embed), F32),
        ((2, half, pair, embed), BF16),
        ((2, half, pair, embed), BF16),
        ((rows, embed), BF16),
        ((rows, embed), BF16),
        halves,
        halves,
        halves,
        ((2, group, part_rows, lanes), BF16),
        ((2, group, part_rows, lanes), BF16),
        ((2, whalf, embed), F32),
        ((whalf, embed), BF16),
        ((whalf, embed), BF16),
        ((zs, part, embed), BF16),
        ((zs, part, embed), BF16),
        ((part, embed), BF16),
        ((part, embed), BF16),
        ((2, zs, part, embed), BF16),
    ]
    shapes = (
        jax.ShapeDtypeStruct((rows, embed), F32),
        jax.ShapeDtypeStruct((rows, width), BF16),
        jax.ShapeDtypeStruct((wrows, embed), BF16),
    )
    outs = pl.pallas_call(
        functools.partial(kernel, zs, xs),
        out_shape=shapes,
        in_specs=[anywhere] * 3 + [vmem] * 3,
        out_specs=(anywhere,) * 3,
        scratch_shapes=[pltpu.VMEM(shape, kind) for shape, kind in scratch]
        + [pltpu.SemaphoreType.DMA((SEMS,)), pltpu.SemaphoreType.DMA((SEMS,)), pltpu.SemaphoreType.DMA((3,))],
        compiler_params=pltpu.CompilerParams(
            collective_id=0, has_side_effects=True, vmem_limit_bytes=56 * 2**20
        ),
    )(
        feats,
        proj_weight,
        text_emb,
        partner.reshape(1, group * rows),
        log_scale.reshape(1, 1),
        bias.reshape(1, 1),
    )
    return pl.pallas_call(
        move,
        out_shape=shapes[:2] + (jax.ShapeDtypeStruct((wrows, embed), F32),),
        in_specs=[vmem] * 3,
        out_specs=(vmem,) * 3,
    )(*outs)


def solution(mesh):
    zs = mesh.shape["dp"] // 4
    xs = mesh.shape["fsdp"] // 2
    return jax.shard_map(
        functools.partial(body, zs, xs),
        mesh=mesh,
        in_specs=(
            P(("dp", "fsdp"), None),
            P("fsdp", None),
            P(("dp", "fsdp"), None),
            P("dp"),
            P(),
            P(),
        ),
        out_specs=(P(("dp", "fsdp"), None), P(("dp", "fsdp"), None), P("fsdp", None)),
        check_vma=False,
    )
```

```python
import functools

import jax
import jax.numpy as jnp
from jax import lax
from jax.experimental import pallas as pl
from jax.experimental.pallas import tpu as pltpu
from jax.sharding import PartitionSpec as P

NORM_EPS = 1e-06
MESH = pl.DeviceIdType.MESH
F32 = jnp.float32
BF16 = jnp.bfloat16
NT = (((1,), (1,)), ((), ()))


def normalize(values):
    inverse = lax.rsqrt(jnp.sum(values * values, axis=-1, keepdims=True) + NORM_EPS)
    return (values * inverse, inverse)


def kernel(
    zs,
    xs,
    feats_in,
    wshard_in,
    text_in,
    partner,
    log_scale,
    bias,
    grad_text_out,
    grad_feats_out,
    grad_weight_out,
    feats,
    wshard,
    text_emb,
    grad_text,
    grad_feats,
    grad_weight,
    texts,
    images,
    fsplit,
    fgroup,
    fturned,
    pacc,
    pout,
    pin,
    pmid,
    pin_y,
    pback,
    proj,
    pbuf,
    wbuf,
    tpart,
    tsib,
    image_acc,
    ring_in,
    ring_out,
    yout,
    yin,
    iout,
    iin,
    grads,
    gfout,
    gfin,
    gw,
    gout,
    gsib,
    zout,
    zin,
    gyout,
    gyin,
    fin,
    send,
    recv,
    local,
):
    rows, embed = text_emb.shape
    wrows = wshard.shape[0]
    whalf = wrows // 2
    group = 2 * xs
    part_rows = rows // 2
    image_half = group * part_rows
    pair = 2 * rows
    unit = 4 * rows
    half = zs // 2
    p = lax.axis_index("dp")
    f = lax.axis_index("fsdp")
    core = lax.rem(p, 2)
    z = lax.rem(p // 2, zs)
    yh = p // (2 * zs)
    x = lax.rem(f, xs)
    yl = f // xs

    def at_z(zz):
        return (yh * (2 * zs) + zz * 2 + core, f)

    def zplus(by):
        return lax.rem(z + by + zs, zs)

    sib = (p + 1 - 2 * core, f)
    across = (p + 2 * zs * (1 - 2 * yh), f)

    def peer(k):
        dy, dx = k // xs, k % xs
        to_y = 1 - yl if dy else yl
        return to_y * xs + lax.rem(x + dx, xs)

    used = [0]
    pending = []

    def ids(count):
        first = used[0]
        used[0] += count
        return first

    def copy(src, dst, i, device):
        return pltpu.make_async_remote_copy(
            src_ref=src,
            dst_ref=dst,
            send_sem=send.at[i],
            recv_sem=recv.at[i],
            device_id=device,
            device_id_type=MESH,
        )

    def start(src, dst, i, device):
        c = copy(src, dst, i, device)
        c.start()
        pending.append(c)
        return c

    group_ks = [k for k in (1, xs - 1, xs, 2, xs + 1, 2 * xs - 1, xs + 2) if k < group]
    group_ks = list(dict.fromkeys(group_ks))
    assert len(group_ks) == group - 1

    def to_group(src, dst):
        first = ids(group)
        return [start(src(k), dst(k), first + k, (p, peer(k))) for k in group_ks]

    def wait_all(copies):
        for c in copies:
            c.wait_recv()

    dxs = list(dict.fromkeys([1, xs - 1] + list(range(2, xs - 1))))
    facing = (1 - yl) * xs + x

    def along_x(dx):
        return yl * xs + lax.rem(x + dx + xs, xs)

    def facing_x(dx):
        return (1 - yl) * xs + lax.rem(x + dx + xs, xs)

    def gather_start(buf, h):
        own = buf.at[h, f]
        cy = start(own, own, ids(1), (p, facing))
        return cy, [start(own, own, ids(1), (p, along_x(dx))) for dx in dxs]

    def gather_x_first(buf, h, copies):
        cy, cx = copies
        out = [cy]
        for dx, c in zip(dxs, cx):
            c.wait_recv()
            a = buf.at[h, along_x(-dx)]
            out.append(start(a, a, ids(1), (p, facing)))
        return out

    def gather_y_first(buf, h, copies):
        cy, cx = copies
        cy.wait_recv()
        a = buf.at[h, facing]
        return cx + [start(a, a, ids(1), (p, along_x(dx))) for dx in dxs]

    feats_load = pltpu.make_async_copy(feats_in, feats, local.at[0])
    text_load = pltpu.make_async_copy(text_in, text_emb, local.at[1])
    weight_load = pltpu.make_async_copy(wshard_in, wshard, local.at[2])
    for c in (feats_load, text_load, weight_load):
        c.start()

    barrier = pltpu.get_barrier_semaphore()
    others = [sib, across]
    others += [at_z(zplus(k)) for k in range(1, zs)]
    others += [(p, peer(k)) for k in range(1, group)]
    for device in others:
        pl.semaphore_signal(barrier, inc=1, device_id=device, device_id_type=MESH)

    feats_load.wait()
    fsplit[...] = jnp.zeros_like(fsplit)
    for j in range(group):
        fsplit[j, :, :wrows] = feats[:, j * wrows : (j + 1) * wrows]
    pl.semaphore_wait(barrier, len(others))
    fcopies = to_group(lambda k: fsplit.at[peer(k)], lambda k: fgroup.at[f])

    text_load.wait()
    text_unit, text_inv = normalize(text_emb[...].astype(F32))

    def chunk(q):
        y = yh if q == 0 else 1 - yh
        return pl.ds(pl.multiple_of(core * pair + y * rows, 16), rows)

    texts[z, chunk(0)] = text_unit.astype(BF16)
    own_text = texts.at[z, chunk(0)]
    ty = start(own_text, own_text, ids(1), across)
    ring = {}
    text_sib = {}

    def ring_send(way, s, q):
        u = zplus(-way * s)
        a = texts.at[u, chunk(q)]
        ring[way, s, q] = start(a, a, ids(1), at_z(zplus(way)))

    def to_sib(by, q):
        a = texts.at[zplus(by), chunk(q)]
        text_sib.setdefault(by, []).append(start(a, a, ids(1), sib))

    def arrive(s, q):
        for way in (1, -1):
            if (way, s, q) not in ring:
                continue
            ring[way, s, q].wait_recv()
            if s < half - 2 or (s == half - 2 and q == (0 if way == 1 else 1)):
                ring_send(way, s + 1, q)
            by = -way * (s + 1)
            to_sib(half if by == -half else by, q)

    def text_ready(by):
        wait_all(text_sib[by])

    ring_send(1, 0, 0)
    ring_send(-1, 0, 0)
    to_sib(0, 0)

    fgroup[f] = fsplit[f]
    gfout[...] = jnp.zeros_like(gfout)
    for h in range(2):
        for j in range(group):
            lane = j * rows + h * part_rows
            pbuf[h, :, j * part_rows : (j + 1) * part_rows] = partner[:, lane : lane + part_rows]
    image_acc[...] = jnp.zeros_like(image_acc)

    weight_load.wait()
    wait_all(fcopies)
    pcopies = []

    def own_block(ref, h, j):
        return ref[h, pl.ds(pl.multiple_of(j * part_rows, 16), part_rows)]

    def sums_start_x():
        relay = [start(pout.at[0, facing_x(dx)], pmid.at[i], ids(1), (p, along_x(dx))) for i, dx in enumerate(dxs)]
        final = [start(pout.at[0, along_x(dx)], pin.at[0, i], ids(1), (p, along_x(dx))) for i, dx in enumerate(dxs)]
        return relay, final

    def sums_start_y():
        return [start(pout.at[1, facing_x(dx)], pin_y.at[i], ids(1), (p, facing)) for i, dx in enumerate(dxs + [0])]

    for h in range(2):
        cols = fgroup[:, h * part_rows : (h + 1) * part_rows, :wrows].reshape(image_half, wrows)
        pacc[h] = jnp.dot(cols, wshard[...], preferred_element_type=F32)
        pout[h] = pacc[h].reshape(group, part_rows, embed).astype(BF16)
        pcopies.append(sums_start_y() if h else sums_start_x())
        if h == 0:
            arrive(0, 0)
    ty.wait_recv()
    ring_send(1, 0, 1)
    ring_send(-1, 0, 1)
    to_sib(0, 1)
    arrive(1, 0)
    for h in range(2):
        cols = fgroup[:, h * part_rows : (h + 1) * part_rows, :wrows].reshape(image_half, wrows)
        fturned[h] = cols.T
    relay, final0 = pcopies[0]
    wait_all(relay)
    total = own_block(pacc, 0, facing)
    for i in range(len(dxs)):
        total += pmid[i].astype(F32)
    pback[0] = total.astype(BF16)
    final0.append(start(pback.at[0], pin.at[0, len(dxs)], ids(1), (p, facing)))
    arrive(0, 1)
    final1 = []
    for i, dx in enumerate(dxs):
        pcopies[1][i].wait_recv()
        pback[1 + i] = (own_block(pacc, 1, along_x(dx)) + pin_y[i].astype(F32)).astype(BF16)
        final1.append(start(pback.at[1 + i], pin.at[1, i], ids(1), (p, along_x(dx))))

    def project(h, copies):
        total = own_block(pacc, h, f)
        wait_all(copies)
        if h:
            pcopies[1][len(dxs)].wait_recv()
            total += pin_y[len(dxs)].astype(F32)
        for i in range(len(copies)):
            total += pin[h, i].astype(F32)
        proj[h] = total
        images[h, f] = normalize(total)[0].astype(BF16)
        return gather_start(images, h)

    first = project(0, final0)
    arrive(2, 0)
    second_half = project(1, final1)
    arrive(1, 1)
    icopies = [gather_x_first(images, 0, first)]
    icopies.append(gather_y_first(images, 1, second_half))
    arrive(3, 0)
    arrive(2, 1)

    scale = jnp.exp(log_scale[...])
    half_scale = 0.5 * scale
    half_shift = 0.5 * bias[...]

    def weigh(u, h, block):
        image_rows = images[h].reshape(image_half, embed)
        dots = lax.dot_general(block, image_rows, NT, preferred_element_type=F32)
        r = lax.broadcasted_iota(jnp.int32, (unit, 1), 0)
        c_of = r // pair
        y_of = lax.rem(r // rows, 2)
        index = ((y_of * (2 * zs) + u * 2 + c_of) * group + f) * rows + lax.rem(r, rows)
        level = jnp.where(pbuf[h] == index, F32(-0.5), F32(0.5))
        weight = (0.5 * jnp.tanh(half_scale * dots + half_shift) + level).astype(BF16)
        wbuf[u, :, h * image_half : (h + 1) * image_half] = weight
        return weight

    def front(units, h):
        blocks = [texts[u] for u in units]
        weights = [weigh(u, h, block) for u, block in zip(units, blocks)]
        total = jnp.dot(weights[0].T, blocks[0], preferred_element_type=F32)
        for weight, block in zip(weights[1:], blocks[1:]):
            total += jnp.dot(weight.T, block, preferred_element_type=F32)
        image_acc[h] += total

    iscopies = []

    def image_sums(h):
        iout[h] = image_acc[h].reshape(group, part_rows, embed).astype(BF16)
        iscopies.append(to_group(lambda k: iout.at[h, peer(k)], lambda k: iin.at[h, k]))

    text_ready(0)
    wait_all(icopies[0])
    front([z], 0)
    for s in range(1, half):
        if s == half - 1:
            arrive(s, 1)
        text_ready(-s)
        text_ready(s)
        front([zplus(-s), zplus(s)], 0)
    text_ready(half)
    front([zplus(half)], 0)
    image_sums(0)
    wait_all(icopies[1])

    def second(i, carry):
        front([2 * i, 2 * i + 1], 1)
        return carry

    lax.fori_loop(0, zs // 2, second, 0)
    image_sums(1)

    tpid = ids(zs)
    sib_pair = pl.ds(pl.multiple_of((1 - core) * pair, 16), pair)

    def part_copy(k):
        return copy(tpart.at[k, sib_pair], tsib.at[k], tpid + k, sib)

    def back(k, carry):
        d = half - (k + 1) // 2
        u = lax.rem(z + jnp.where(lax.rem(k, 2) == 1, d, zs - d), zs)
        image_rows = images[...].reshape(2 * image_half, embed)
        tpart[k] = jnp.dot(wbuf[u], image_rows, preferred_element_type=F32).astype(BF16)
        part_copy(k).start()
        return carry

    sum_r, sum_l = {}, {}

    def own_sum(k, lo, count):
        at = pl.ds(pl.multiple_of(core * pair + lo, 16), count)
        return tpart[k, at].astype(F32) + tsib[k, lo : lo + count].astype(F32)

    def sum_step(s):
        kr, kl = (0, 0) if s == 0 else (2 * s - 1, 2 * s)
        for k in range(0 if s == 0 else kr, kl + 1):
            part_copy(k).wait_recv()
        for q in range(2):
            at = pl.ds(q * rows, rows)
            for way, sums, k, step in ((0, sum_r, kr, 1), (1, sum_l, kl, -1)):
                if s == 0 and q != way:
                    continue
                total = own_sum(k, q * rows, rows)
                if (s - 1, q) in sums:
                    sums[s - 1, q].wait_recv()
                    total += ring_in[way, s - 1, at].astype(F32)
                ring_out[way, s, at] = total.astype(BF16)
                sums[s, q] = start(
                    ring_out.at[way, s, at], ring_in.at[way, s, at], ids(1), at_z(zplus(step))
                )

    lax.fori_loop(0, 2, back, 0)
    sum_step(0)
    lax.fori_loop(2, zs, back, 0, unroll=2)


    def project_back(h):
        total = own_block(image_acc, h, f)
        wait_all(iscopies[h])
        for k in group_ks:
            total += iin[h, k].astype(F32)
        image_dir = scale * total
        image_unit, image_inv = normalize(proj[h])
        along = jnp.sum(image_unit * image_dir, axis=-1, keepdims=True)
        grads[h, f] = (image_inv * (image_dir - image_unit * along)).astype(BF16)
        return gather_start(grads, h)

    first = project_back(0)
    sum_step(1)
    second_half = project_back(1)
    gcopies = [gather_x_first(grads, 0, first)]
    gcopies.append(gather_y_first(grads, 1, second_half))
    sum_step(2)

    own_half = pl.ds(pl.multiple_of(core * whalf, 16), whalf)
    other_half = pl.ds(pl.multiple_of((1 - core) * whalf, 16), whalf)
    part = zout.shape[1]
    used_parts = whalf // part
    for j in range(used_parts, zs):
        zout[j] = jnp.zeros_like(zout[j])
    middle = (embed // 128 + 1) // 2 * 128
    cuts = [slice(0, middle), slice(middle, embed)]

    def weight_part(h, at, cut):
        some = grads[h, :, :, cut].reshape(image_half, cut.stop - cut.start)
        return jnp.dot(fturned[h, at], some, preferred_element_type=F32)

    wait_all(gcopies[0])
    for cut in cuts:
        gw[0, :, cut] = weight_part(0, other_half, cut)
        gw[1, :, cut] = weight_part(0, own_half, cut)
    wait_all(gcopies[1])
    gs = []
    for cut in cuts:
        gout[:, cut] = (gw[0, :, cut] + weight_part(1, other_half, cut)).astype(BF16)
        gs.append(start(gout.at[:, cut], gsib.at[:, cut], ids(1), sib))
        gw[1, :, cut] += weight_part(1, own_half, cut)
    zcopies = []
    for cut, c in zip(cuts, gs):
        c.wait_recv()
        total = (gw[1, :, cut] + gsib[:, cut].astype(F32)).astype(BF16)
        zout[:used_parts, :, cut] = total.reshape(used_parts, part, cut.stop - cut.start)
        zcopies.append(
            [
                start(zout.at[zplus(k), :, cut], zin.at[k, :, cut], ids(1), at_z(zplus(k)))
                for k in range(1, zs)
            ]
        )

    gfcopies = []
    for h in range(2):
        cols = lax.dot_general(
            grads[h].reshape(image_half, embed), wshard[...], NT, preferred_element_type=F32
        )
        gfout[h, :, :, :wrows] = cols.astype(BF16).reshape(group, part_rows, wrows)
        gfcopies += to_group(lambda k: gfout.at[h, peer(k)], lambda k: gfin.at[h, f])
        gfin[h, f] = gfout[h, f]
    for s in range(3, half):
        sum_step(s)

    gy = []
    for cut, copies in zip(cuts, zcopies):
        weight_sum = zout[z, :, cut].astype(F32)
        for k, c in zip(range(1, zs), copies):
            c.wait_recv()
            weight_sum += zin[k, :, cut].astype(F32)
        gyout[:, cut] = weight_sum.astype(BF16)
        gy.append(start(gyout.at[:, cut], gyin.at[:, cut], ids(1), across))
    fincopies = []
    for cut, c in zip(cuts, gy):
        c.wait_recv()
        fin[core, z, :, cut] = (
            gyout[:, cut].astype(F32) + gyin[:, cut].astype(F32)
        ).astype(BF16)
        own = fin.at[core, z, :, cut]
        fincopies.append([start(own, own, ids(1), at_z(zplus(k))) for k in range(1, zs)])
    wait_all(gfcopies)
    for h in range(2):
        for j in range(group):
            at = (slice(h * part_rows, (h + 1) * part_rows), slice(j * wrows, (j + 1) * wrows))
            grad_feats[at] = gfin[h, j, :, :wrows]
    feats_store = pltpu.make_async_copy(grad_feats, grad_feats_out, local.at[0])
    feats_store.start()

    part_copy(zs - 1).wait_recv()
    for q in range(2):
        sum_r[half - 1, q].wait_recv()
        sum_l[half - 1, q].wait_recv()
    theirs = pl.ds(pl.multiple_of((1 - yh) * rows, 16), rows)
    ours = pl.ds(pl.multiple_of(yh * rows, 16), rows)

    def gathered(at, lo):
        here = pl.ds(pl.multiple_of(core * pair + lo, 16), rows)
        return (
            (tpart[zs - 1, here].astype(F32) + tsib[zs - 1, at].astype(F32))
            + (ring_in[0, half - 1, at].astype(F32) + ring_in[1, half - 1, at].astype(F32))
        )

    yout[...] = gathered(theirs, (1 - yh) * rows).astype(BF16)
    yc = start(yout, yin, ids(1), across)
    fs = []
    for cut, copies in zip(cuts, fincopies):
        wait_all(copies)
        own = fin.at[core, :, :, cut]
        fs.append(start(own, own, ids(1), sib))
    yc.wait_recv()
    text_dir = scale * (gathered(ours, yh * rows) + yin[...].astype(F32))
    text_unit, text_inv = normalize(text_emb[...].astype(F32))
    along = jnp.sum(text_unit * text_dir, axis=-1, keepdims=True)
    grad_text[...] = text_inv * (text_dir - text_unit * along)
    text_store = pltpu.make_async_copy(grad_text, grad_text_out, local.at[1])
    text_store.start()
    wait_all(fs)
    for c in range(2):
        grad_weight[c * whalf : (c + 1) * whalf] = (
            fin[c, :used_parts].reshape(whalf, embed)
        )
    weight_store = pltpu.make_async_copy(grad_weight, grad_weight_out, local.at[2])
    weight_store.start()

    for c in pending:
        c.wait_send()

    def part_done(k, carry):
        part_copy(k).wait_send()
        return carry

    lax.fori_loop(0, zs, part_done, 0)
    feats_store.wait()
    text_store.wait()
    weight_store.wait()


SEMS = 256


def move(a, b, c, x, y, z):
    z[...] = c[...].astype(F32)
    x[...] = a[...]
    y[...] = b[...]


def body(zs, xs, feats, proj_weight, text_emb, partner, log_scale, bias):
    rows, width = feats.shape
    wrows, embed = proj_weight.shape
    group = 2 * xs
    pair, unit = 2 * rows, 4 * rows
    half = zs // 2
    whalf = wrows // 2
    part_rows = rows // 2
    image_half = group * part_rows
    lanes = -(-wrows // 128) * 128
    part = -(-whalf // zs // 16) * 16
    vmem = pl.BlockSpec(memory_space=pltpu.VMEM)
    anywhere = pl.BlockSpec(memory_space=pl.ANY)
    halves = ((2, group, part_rows, embed), BF16)
    scratch = [
        ((rows, width), BF16),
        ((wrows, embed), BF16),
        ((rows, embed), BF16),
        ((rows, embed), F32),
        ((rows, width), BF16),
        ((wrows, embed), BF16),
        ((zs, unit, embed), BF16),
        halves,
        ((group, rows, lanes), BF16),
        ((group, rows, lanes), BF16),
        ((2, wrows, image_half), BF16),
        ((2, image_half, embed), F32),
        halves,
        ((2, group // 2, part_rows, embed), BF16),
        ((group // 2, part_rows, embed), BF16),
        ((group // 2, part_rows, embed), BF16),
        ((group // 2, part_rows, embed), BF16),
        ((2, part_rows, embed), F32),
        ((2, 1, image_half), jnp.int32),
        ((zs, unit, 2 * image_half), BF16),
        ((zs, unit, embed), BF16),
        ((zs, pair, embed), BF16),
        ((2, image_half, embed), F32),
        ((2, half, pair, embed), BF16),
        ((2, half, pair, embed), BF16),
        ((rows, embed), BF16),
        ((rows, embed), BF16),
        halves,
        halves,
        halves,
        ((2, group, part_rows, lanes), BF16),
        ((2, group, part_rows, lanes), BF16),
        ((2, whalf, embed), F32),
        ((whalf, embed), BF16),
        ((whalf, embed), BF16),
        ((zs, part, embed), BF16),
        ((zs, part, embed), BF16),
        ((part, embed), BF16),
        ((part, embed), BF16),
        ((2, zs, part, embed), BF16),
    ]
    shapes = (
        jax.ShapeDtypeStruct((rows, embed), F32),
        jax.ShapeDtypeStruct((rows, width), BF16),
        jax.ShapeDtypeStruct((wrows, embed), BF16),
    )
    outs = pl.pallas_call(
        functools.partial(kernel, zs, xs),
        out_shape=shapes,
        in_specs=[anywhere] * 3 + [vmem] * 3,
        out_specs=(anywhere,) * 3,
        scratch_shapes=[pltpu.VMEM(shape, kind) for shape, kind in scratch]
        + [pltpu.SemaphoreType.DMA((SEMS,)), pltpu.SemaphoreType.DMA((SEMS,)), pltpu.SemaphoreType.DMA((3,))],
        compiler_params=pltpu.CompilerParams(
            collective_id=0, has_side_effects=True, vmem_limit_bytes=56 * 2**20
        ),
    )(
        feats,
        proj_weight,
        text_emb,
        partner.reshape(1, group * rows),
        log_scale.reshape(1, 1),
        bias.reshape(1, 1),
    )
    return pl.pallas_call(
        move,
        out_shape=shapes[:2] + (jax.ShapeDtypeStruct((wrows, embed), F32),),
        in_specs=[vmem] * 3,
        out_specs=(vmem,) * 3,
    )(*outs)


def solution(mesh):
    zs = mesh.shape["dp"] // 4
    xs = mesh.shape["fsdp"] // 2
    return jax.shard_map(
        functools.partial(body, zs, xs),
        mesh=mesh,
        in_specs=(
            P(("dp", "fsdp"), None),
            P("fsdp", None),
            P(("dp", "fsdp"), None),
            P("dp"),
            P(),
            P(),
        ),
        out_specs=(P(("dp", "fsdp"), None), P(("dp", "fsdp"), None), P("fsdp", None)),
        check_vma=False,
    )
```

```python
import functools

import jax
import jax.numpy as jnp
from jax import lax
from jax.experimental import pallas as pl
from jax.experimental.pallas import tpu as pltpu
from jax.sharding import PartitionSpec as P

NORM_EPS = 1e-06
MESH = pl.DeviceIdType.MESH
F32 = jnp.float32
BF16 = jnp.bfloat16
NT = (((1,), (1,)), ((), ()))


def normalize(values):
    inverse = lax.rsqrt(jnp.sum(values * values, axis=-1, keepdims=True) + NORM_EPS)
    return (values * inverse, inverse)


def kernel(
    zs,
    xs,
    feats_in,
    wshard_in,
    text_in,
    partner,
    log_scale,
    bias,
    grad_text_out,
    grad_feats_out,
    grad_weight_out,
    feats,
    wshard,
    text_emb,
    grad_text,
    grad_feats,
    grad_weight,
    texts,
    images,
    fsplit,
    fgroup,
    fturned,
    pacc,
    pout,
    pin,
    pmid,
    pin_y,
    pback,
    proj,
    pbuf,
    wbuf,
    tpart,
    tsib,
    image_acc,
    ring_in,
    ring_out,
    yout,
    yin,
    iout,
    iin,
    grads,
    gfout,
    gfin,
    gw,
    gout,
    gsib,
    zout,
    zin,
    gyout,
    gyin,
    fin,
    send,
    recv,
    local,
):
    rows, embed = text_emb.shape
    wrows = wshard.shape[0]
    whalf = wrows // 2
    group = 2 * xs
    part_rows = rows // 2
    image_half = group * part_rows
    pair = 2 * rows
    unit = 4 * rows
    half = zs // 2
    p = lax.axis_index("dp")
    f = lax.axis_index("fsdp")
    core = lax.rem(p, 2)
    z = lax.rem(p // 2, zs)
    yh = p // (2 * zs)
    x = lax.rem(f, xs)
    yl = f // xs

    def at_z(zz):
        return (yh * (2 * zs) + zz * 2 + core, f)

    def zplus(by):
        return lax.rem(z + by + zs, zs)

    sib = (p + 1 - 2 * core, f)
    across = (p + 2 * zs * (1 - 2 * yh), f)

    def peer(k):
        dy, dx = k // xs, k % xs
        to_y = 1 - yl if dy else yl
        return to_y * xs + lax.rem(x + dx, xs)

    used = [0]
    pending = []

    def ids(count):
        first = used[0]
        used[0] += count
        return first

    def copy(src, dst, i, device):
        return pltpu.make_async_remote_copy(
            src_ref=src,
            dst_ref=dst,
            send_sem=send.at[i],
            recv_sem=recv.at[i],
            device_id=device,
            device_id_type=MESH,
        )

    def start(src, dst, i, device):
        c = copy(src, dst, i, device)
        c.start()
        pending.append(c)
        return c

    group_ks = [k for k in (1, xs - 1, xs, 2, xs + 1, 2 * xs - 1, xs + 2) if k < group]
    group_ks = list(dict.fromkeys(group_ks))
    assert len(group_ks) == group - 1

    def to_group(src, dst):
        first = ids(group)
        return [start(src(k), dst(k), first + k, (p, peer(k))) for k in group_ks]

    def wait_all(copies):
        for c in copies:
            c.wait_recv()

    dxs = list(dict.fromkeys([1, xs - 1] + list(range(2, xs - 1))))
    facing = (1 - yl) * xs + x

    def along_x(dx):
        return yl * xs + lax.rem(x + dx + xs, xs)

    def facing_x(dx):
        return (1 - yl) * xs + lax.rem(x + dx + xs, xs)

    def gather_start(buf, h):
        own = buf.at[h, f]
        cy = start(own, own, ids(1), (p, facing))
        return cy, [start(own, own, ids(1), (p, along_x(dx))) for dx in dxs]

    def gather_x_first(buf, h, copies):
        cy, cx = copies
        out = [cy]
        for dx, c in zip(dxs, cx):
            c.wait_recv()
            a = buf.at[h, along_x(-dx)]
            out.append(start(a, a, ids(1), (p, facing)))
        return out

    def gather_y_first(buf, h, copies):
        cy, cx = copies
        cy.wait_recv()
        a = buf.at[h, facing]
        return cx + [start(a, a, ids(1), (p, along_x(dx))) for dx in dxs]

    feats_load = pltpu.make_async_copy(feats_in, feats, local.at[0])
    text_load = pltpu.make_async_copy(text_in, text_emb, local.at[1])
    weight_load = pltpu.make_async_copy(wshard_in, wshard, local.at[2])
    for c in (feats_load, text_load, weight_load):
        c.start()

    barrier = pltpu.get_barrier_semaphore()
    others = [sib, across]
    others += [at_z(zplus(k)) for k in range(1, zs)]
    others += [(p, peer(k)) for k in range(1, group)]
    for device in others:
        pl.semaphore_signal(barrier, inc=1, device_id=device, device_id_type=MESH)

    feats_load.wait()
    fsplit[...] = jnp.zeros_like(fsplit)
    for j in range(group):
        fsplit[j, :, :wrows] = feats[:, j * wrows : (j + 1) * wrows]
    pl.semaphore_wait(barrier, len(others))
    fcopies = to_group(lambda k: fsplit.at[peer(k)], lambda k: fgroup.at[f])

    text_load.wait()
    text_unit, text_inv = normalize(text_emb[...].astype(F32))

    def chunk(q):
        y = yh if q == 0 else 1 - yh
        return pl.ds(pl.multiple_of(core * pair + y * rows, 16), rows)

    texts[z, chunk(0)] = text_unit.astype(BF16)
    own_text = texts.at[z, chunk(0)]
    ty = start(own_text, own_text, ids(1), across)
    ring = {}
    text_sib = {}

    def ring_send(way, s, q):
        u = zplus(-way * s)
        a = texts.at[u, chunk(q)]
        ring[way, s, q] = start(a, a, ids(1), at_z(zplus(way)))

    def to_sib(by, q):
        a = texts.at[zplus(by), chunk(q)]
        text_sib.setdefault(by, []).append(start(a, a, ids(1), sib))

    def arrive(s, q):
        for way in (1, -1):
            if (way, s, q) not in ring:
                continue
            ring[way, s, q].wait_recv()
            if s < half - 2 or (s == half - 2 and q == (0 if way == 1 else 1)):
                ring_send(way, s + 1, q)
            by = -way * (s + 1)
            to_sib(half if by == -half else by, q)

    def text_ready(by):
        wait_all(text_sib[by])

    ring_send(1, 0, 0)
    ring_send(-1, 0, 0)
    to_sib(0, 0)

    fgroup[f] = fsplit[f]
    gfout[...] = jnp.zeros_like(gfout)
    for h in range(2):
        for j in range(group):
            lane = j * rows + h * part_rows
            pbuf[h, :, j * part_rows : (j + 1) * part_rows] = partner[:, lane : lane + part_rows]
    image_acc[...] = jnp.zeros_like(image_acc)

    weight_load.wait()
    wait_all(fcopies)
    pcopies = []

    def own_block(ref, h, j):
        return ref[h, pl.ds(pl.multiple_of(j * part_rows, 16), part_rows)]

    def sums_start_x():
        relay = [start(pout.at[0, facing_x(dx)], pmid.at[i], ids(1), (p, along_x(dx))) for i, dx in enumerate(dxs)]
        final = [start(pout.at[0, along_x(dx)], pin.at[0, i], ids(1), (p, along_x(dx))) for i, dx in enumerate(dxs)]
        return relay, final

    def sums_start_y():
        return [start(pout.at[1, facing_x(dx)], pin_y.at[i], ids(1), (p, facing)) for i, dx in enumerate(dxs + [0])]

    for h in range(2):
        cols = fgroup[:, h * part_rows : (h + 1) * part_rows, :wrows].reshape(image_half, wrows)
        pacc[h] = jnp.dot(cols, wshard[...], preferred_element_type=F32)
        pout[h] = pacc[h].reshape(group, part_rows, embed).astype(BF16)
        pcopies.append(sums_start_y() if h else sums_start_x())
        if h == 0:
            arrive(0, 0)
    ty.wait_recv()
    ring_send(1, 0, 1)
    ring_send(-1, 0, 1)
    to_sib(0, 1)
    arrive(1, 0)
    for h in range(2):
        cols = fgroup[:, h * part_rows : (h + 1) * part_rows, :wrows].reshape(image_half, wrows)
        fturned[h] = cols.T
    relay, final0 = pcopies[0]
    wait_all(relay)
    total = own_block(pacc, 0, facing)
    for i in range(len(dxs)):
        total += pmid[i].astype(F32)
    pback[0] = total.astype(BF16)
    final0.append(start(pback.at[0], pin.at[0, len(dxs)], ids(1), (p, facing)))
    arrive(0, 1)
    final1 = []
    for i, dx in enumerate(dxs):
        pcopies[1][i].wait_recv()
        pback[1 + i] = (own_block(pacc, 1, along_x(dx)) + pin_y[i].astype(F32)).astype(BF16)
        final1.append(start(pback.at[1 + i], pin.at[1, i], ids(1), (p, along_x(dx))))

    def project(h, copies):
        total = own_block(pacc, h, f)
        wait_all(copies)
        if h:
            pcopies[1][len(dxs)].wait_recv()
            total += pin_y[len(dxs)].astype(F32)
        for i in range(len(copies)):
            total += pin[h, i].astype(F32)
        proj[h] = total
        images[h, f] = normalize(total)[0].astype(BF16)
        return gather_start(images, h)

    first = project(0, final0)
    arrive(2, 0)
    second_half = project(1, final1)
    arrive(1, 1)
    icopies = [gather_x_first(images, 0, first)]
    icopies.append(gather_y_first(images, 1, second_half))
    arrive(3, 0)
    arrive(2, 1)

    scale = jnp.exp(log_scale[...])
    half_scale = 0.5 * scale
    half_shift = 0.5 * bias[...]

    def weigh(u, h, block):
        image_rows = images[h].reshape(image_half, embed)
        dots = lax.dot_general(block, image_rows, NT, preferred_element_type=F32)
        r = lax.broadcasted_iota(jnp.int32, (unit, 1), 0)
        c_of = r // pair
        y_of = lax.rem(r // rows, 2)
        index = ((y_of * (2 * zs) + u * 2 + c_of) * group + f) * rows + lax.rem(r, rows)
        level = jnp.where(pbuf[h] == index, F32(-0.5), F32(0.5))
        weight = (0.5 * jnp.tanh(half_scale * dots + half_shift) + level).astype(BF16)
        wbuf[u, :, h * image_half : (h + 1) * image_half] = weight
        return weight

    def front(units, h):
        blocks = [texts[u] for u in units]
        weights = [weigh(u, h, block) for u, block in zip(units, blocks)]
        total = jnp.dot(weights[0].T, blocks[0], preferred_element_type=F32)
        for weight, block in zip(weights[1:], blocks[1:]):
            total += jnp.dot(weight.T, block, preferred_element_type=F32)
        image_acc[h] += total

    iscopies = []

    def image_sums(h):
        iout[h] = image_acc[h].reshape(group, part_rows, embed).astype(BF16)
        iscopies.append(to_group(lambda k: iout.at[h, peer(k)], lambda k: iin.at[h, k]))

    text_ready(0)
    wait_all(icopies[0])
    front([z], 0)
    for s in range(1, half):
        if s == half - 1:
            arrive(s, 1)
        text_ready(-s)
        text_ready(s)
        front([zplus(-s), zplus(s)], 0)
    text_ready(half)
    front([zplus(half)], 0)
    image_sums(0)
    wait_all(icopies[1])

    def second(i, carry):
        front([2 * i, 2 * i + 1], 1)
        return carry

    lax.fori_loop(0, zs // 2, second, 0)
    image_sums(1)

    tpid = ids(zs)
    sib_pair = pl.ds(pl.multiple_of((1 - core) * pair, 16), pair)

    def part_copy(k):
        return copy(tpart.at[k, sib_pair], tsib.at[k], tpid + k, sib)

    def back(k, carry):
        d = half - (k + 1) // 2
        u = lax.rem(z + jnp.where(lax.rem(k, 2) == 1, d, zs - d), zs)
        image_rows = images[...].reshape(2 * image_half, embed)
        tpart[k] = jnp.dot(wbuf[u], image_rows, preferred_element_type=F32).astype(BF16)
        part_copy(k).start()
        return carry

    sum_r, sum_l = {}, {}

    def own_sum(k, lo, count):
        at = pl.ds(pl.multiple_of(core * pair + lo, 16), count)
        return tpart[k, at].astype(F32) + tsib[k, lo : lo + count].astype(F32)

    def sum_step(s):
        kr, kl = (0, 0) if s == 0 else (2 * s - 1, 2 * s)
        for k in range(0 if s == 0 else kr, kl + 1):
            part_copy(k).wait_recv()
        for q in range(2):
            at = pl.ds(q * rows, rows)
            for way, sums, k, step in ((0, sum_r, kr, 1), (1, sum_l, kl, -1)):
                if s == 0 and q != way:
                    continue
                total = own_sum(k, q * rows, rows)
                if (s - 1, q) in sums:
                    sums[s - 1, q].wait_recv()
                    total += ring_in[way, s - 1, at].astype(F32)
                ring_out[way, s, at] = total.astype(BF16)
                sums[s, q] = start(
                    ring_out.at[way, s, at], ring_in.at[way, s, at], ids(1), at_z(zplus(step))
                )

    lax.fori_loop(0, 2, back, 0)
    sum_step(0)
    lax.fori_loop(2, zs, back, 0, unroll=2)


    def project_back(h):
        total = own_block(image_acc, h, f)
        wait_all(iscopies[h])
        for k in group_ks:
            total += iin[h, k].astype(F32)
        image_dir = scale * total
        image_unit, image_inv = normalize(proj[h])
        along = jnp.sum(image_unit * image_dir, axis=-1, keepdims=True)
        grads[h, f] = (image_inv * (image_dir - image_unit * along)).astype(BF16)
        return gather_start(grads, h)

    first = project_back(0)
    sum_step(1)
    second_half = project_back(1)
    gcopies = [gather_x_first(grads, 0, first)]
    gcopies.append(gather_y_first(grads, 1, second_half))
    sum_step(2)

    own_half = pl.ds(pl.multiple_of(core * whalf, 16), whalf)
    other_half = pl.ds(pl.multiple_of((1 - core) * whalf, 16), whalf)
    part = zout.shape[1]
    used_parts = whalf // part
    for j in range(used_parts, zs):
        zout[j] = jnp.zeros_like(zout[j])
    middle = (embed // 128 + 1) // 2 * 128
    cuts = [slice(0, middle), slice(middle, embed)]

    def weight_part(h, at, cut):
        some = grads[h, :, :, cut].reshape(image_half, cut.stop - cut.start)
        return jnp.dot(fturned[h, at], some, preferred_element_type=F32)

    wait_all(gcopies[0])
    for cut in cuts:
        gw[0, :, cut] = weight_part(0, other_half, cut)
        gw[1, :, cut] = weight_part(0, own_half, cut)
    wait_all(gcopies[1])
    gs = []
    for cut in cuts:
        gout[:, cut] = (gw[0, :, cut] + weight_part(1, other_half, cut)).astype(BF16)
        gs.append(start(gout.at[:, cut], gsib.at[:, cut], ids(1), sib))
        gw[1, :, cut] += weight_part(1, own_half, cut)
    zcopies = []
    for cut, c in zip(cuts, gs):
        c.wait_recv()
        total = (gw[1, :, cut] + gsib[:, cut].astype(F32)).astype(BF16)
        zout[:used_parts, :, cut] = total.reshape(used_parts, part, cut.stop - cut.start)
        zcopies.append(
            [
                start(zout.at[zplus(k), :, cut], zin.at[k, :, cut], ids(1), at_z(zplus(k)))
                for k in range(1, zs)
            ]
        )

    for s in range(3, half):
        sum_step(s)

    gfcopies = []
    for h in range(2):
        cols = lax.dot_general(
            grads[h].reshape(image_half, embed), wshard[...], NT, preferred_element_type=F32
        )
        gfout[h, :, :, :wrows] = cols.astype(BF16).reshape(group, part_rows, wrows)
        gfcopies += to_group(lambda k: gfout.at[h, peer(k)], lambda k: gfin.at[h, f])
        gfin[h, f] = gfout[h, f]

    gy = []
    for cut, copies in zip(cuts, zcopies):
        weight_sum = zout[z, :, cut].astype(F32)
        for k, c in zip(range(1, zs), copies):
            c.wait_recv()
            weight_sum += zin[k, :, cut].astype(F32)
        gyout[:, cut] = weight_sum.astype(BF16)
        gy.append(start(gyout.at[:, cut], gyin.at[:, cut], ids(1), across))
    fincopies = []
    for cut, c in zip(cuts, gy):
        c.wait_recv()
        fin[core, z, :, cut] = (
            gyout[:, cut].astype(F32) + gyin[:, cut].astype(F32)
        ).astype(BF16)
        own = fin.at[core, z, :, cut]
        fincopies.append([start(own, own, ids(1), at_z(zplus(k))) for k in range(1, zs)])
    wait_all(gfcopies)
    for h in range(2):
        for j in range(group):
            at = (slice(h * part_rows, (h + 1) * part_rows), slice(j * wrows, (j + 1) * wrows))
            grad_feats[at] = gfin[h, j, :, :wrows]
    feats_store = pltpu.make_async_copy(grad_feats, grad_feats_out, local.at[0])
    feats_store.start()

    part_copy(zs - 1).wait_recv()
    for q in range(2):
        sum_r[half - 1, q].wait_recv()
        sum_l[half - 1, q].wait_recv()
    theirs = pl.ds(pl.multiple_of((1 - yh) * rows, 16), rows)
    ours = pl.ds(pl.multiple_of(yh * rows, 16), rows)

    def gathered(at, lo):
        here = pl.ds(pl.multiple_of(core * pair + lo, 16), rows)
        return (
            (tpart[zs - 1, here].astype(F32) + tsib[zs - 1, at].astype(F32))
            + (ring_in[0, half - 1, at].astype(F32) + ring_in[1, half - 1, at].astype(F32))
        )

    yout[...] = gathered(theirs, (1 - yh) * rows).astype(BF16)
    yc = start(yout, yin, ids(1), across)
    fs = []
    for cut, copies in zip(cuts, fincopies):
        wait_all(copies)
        own = fin.at[core, :, :, cut]
        fs.append(start(own, own, ids(1), sib))
    yc.wait_recv()
    text_dir = scale * (gathered(ours, yh * rows) + yin[...].astype(F32))
    text_unit, text_inv = normalize(text_emb[...].astype(F32))
    along = jnp.sum(text_unit * text_dir, axis=-1, keepdims=True)
    grad_text[...] = text_inv * (text_dir - text_unit * along)
    text_store = pltpu.make_async_copy(grad_text, grad_text_out, local.at[1])
    text_store.start()
    wait_all(fs)
    for c in range(2):
        grad_weight[c * whalf : (c + 1) * whalf] = (
            fin[c, :used_parts].reshape(whalf, embed)
        )
    weight_store = pltpu.make_async_copy(grad_weight, grad_weight_out, local.at[2])
    weight_store.start()

    for c in pending:
        c.wait_send()

    def part_done(k, carry):
        part_copy(k).wait_send()
        return carry

    lax.fori_loop(0, zs, part_done, 0)
    feats_store.wait()
    text_store.wait()
    weight_store.wait()


SEMS = 256


def move(a, b, c, x, y, z):
    z[...] = c[...].astype(F32)
    x[...] = a[...]
    y[...] = b[...]


def body(zs, xs, feats, proj_weight, text_emb, partner, log_scale, bias):
    rows, width = feats.shape
    wrows, embed = proj_weight.shape
    group = 2 * xs
    pair, unit = 2 * rows, 4 * rows
    half = zs // 2
    whalf = wrows // 2
    part_rows = rows // 2
    image_half = group * part_rows
    lanes = -(-wrows // 128) * 128
    part = -(-whalf // zs // 16) * 16
    vmem = pl.BlockSpec(memory_space=pltpu.VMEM)
    anywhere = pl.BlockSpec(memory_space=pl.ANY)
    halves = ((2, group, part_rows, embed), BF16)
    scratch = [
        ((rows, width), BF16),
        ((wrows, embed), BF16),
        ((rows, embed), BF16),
        ((rows, embed), F32),
        ((rows, width), BF16),
        ((wrows, embed), BF16),
        ((zs, unit, embed), BF16),
        halves,
        ((group, rows, lanes), BF16),
        ((group, rows, lanes), BF16),
        ((2, wrows, image_half), BF16),
        ((2, image_half, embed), F32),
        halves,
        ((2, group // 2, part_rows, embed), BF16),
        ((group // 2, part_rows, embed), BF16),
        ((group // 2, part_rows, embed), BF16),
        ((group // 2, part_rows, embed), BF16),
        ((2, part_rows, embed), F32),
        ((2, 1, image_half), jnp.int32),
        ((zs, unit, 2 * image_half), BF16),
        ((zs, unit, embed), BF16),
        ((zs, pair, embed), BF16),
        ((2, image_half, embed), F32),
        ((2, half, pair, embed), BF16),
        ((2, half, pair, embed), BF16),
        ((rows, embed), BF16),
        ((rows, embed), BF16),
        halves,
        halves,
        halves,
        ((2, group, part_rows, lanes), BF16),
        ((2, group, part_rows, lanes), BF16),
        ((2, whalf, embed), F32),
        ((whalf, embed), BF16),
        ((whalf, embed), BF16),
        ((zs, part, embed), BF16),
        ((zs, part, embed), BF16),
        ((part, embed), BF16),
        ((part, embed), BF16),
        ((2, zs, part, embed), BF16),
    ]
    shapes = (
        jax.ShapeDtypeStruct((rows, embed), F32),
        jax.ShapeDtypeStruct((rows, width), BF16),
        jax.ShapeDtypeStruct((wrows, embed), BF16),
    )
    outs = pl.pallas_call(
        functools.partial(kernel, zs, xs),
        out_shape=shapes,
        in_specs=[anywhere] * 3 + [vmem] * 3,
        out_specs=(anywhere,) * 3,
        scratch_shapes=[pltpu.VMEM(shape, kind) for shape, kind in scratch]
        + [pltpu.SemaphoreType.DMA((SEMS,)), pltpu.SemaphoreType.DMA((SEMS,)), pltpu.SemaphoreType.DMA((3,))],
        compiler_params=pltpu.CompilerParams(
            collective_id=0, has_side_effects=True, vmem_limit_bytes=56 * 2**20
        ),
    )(
        feats,
        proj_weight,
        text_emb,
        partner.reshape(1, group * rows),
        log_scale.reshape(1, 1),
        bias.reshape(1, 1),
    )
    return pl.pallas_call(
        move,
        out_shape=shapes[:2] + (jax.ShapeDtypeStruct((wrows, embed), F32),),
        in_specs=[vmem] * 3,
        out_specs=(vmem,) * 3,
    )(*outs)


def solution(mesh):
    zs = mesh.shape["dp"] // 4
    xs = mesh.shape["fsdp"] // 2
    return jax.shard_map(
        functools.partial(body, zs, xs),
        mesh=mesh,
        in_specs=(
            P(("dp", "fsdp"), None),
            P("fsdp", None),
            P(("dp", "fsdp"), None),
            P("dp"),
            P(),
            P(),
        ),
        out_specs=(P(("dp", "fsdp"), None), P(("dp", "fsdp"), None), P("fsdp", None)),
        check_vma=False,
    )
```
